32 devices in a mesh: groups: 2 (over y), hid: 16 (over z, x, core).
Axes of the slice: x: 2, y: 2, z: 4, core: 2. Of those that a mesh axis runs over, the one named last changes fastest.
Arguments:
- tokens: bfloat16 [4096, 8192], P(('groups', 'hid')), parts along dimension 0, may hold values from -6 to 6
- cotangent: bfloat16 [4096, 8192], P(('groups', 'hid')), parts along dimension 0, may hold values from -5 to 5
- gate_weight: bfloat16 [8192, 2048], P(None, 'hid'), may hold values from -0.0625 to 0.0625
- up_weight: bfloat16 [8192, 2048], P(None, 'hid'), may hold values from -0.0625 to 0.0625
- down_weight: bfloat16 [2048, 8192], P('hid'), may hold values from -0.375 to 0.375
- adapter_input_maps: float32 [16, 16, 2048], P('groups', None, 'hid'), parts along dimension 0, may hold values from -0.375 to 0.375
- adapter_output_maps: float32 [16, 16, 8192], P('groups', None, 'hid'), parts along dimension 0, may hold values from -1.5 to 1.5
- first_moment_input: float32 [16, 16, 2048], P('groups', None, 'hid'), parts along dimension 0, may hold values from -6 to 6
- second_moment_input: float32 [16, 16, 2048], P('groups', None, 'hid'), parts along dimension 0, may hold values from 0.1 to 2
- first_moment_output: float32 [16, 16, 8192], P('groups', None, 'hid'), parts along dimension 0, may hold values from -6 to 6
- second_moment_output: float32 [16, 16, 8192], P('groups', None, 'hid'), parts along dimension 0, may hold values from 0.1 to 2
- active: int32 [32, 2], P('groups'), parts along dimension 0, may hold values from 0 to 15, all different within a row; in each aligned block of 16 rows (0 to 15, 16 to 31, ...) at most 4 rows name the same one
- counts: int32 [32], P('groups'), parts along dimension 0, may hold values from 1 to 2
- dropout_tiles: int32 [4, 128, 128], replicated, may hold values 0 or 1
- seeds: int32 [16], P('groups'), parts along dimension 0, may hold values from 0 to 3
Outputs:
- output: bfloat16 [4096, 8192], P(('groups', 'hid')), parts along dimension 0
- updated_input_maps: float32 [16, 16, 2048], P('groups', None, 'hid'), parts along dimension 0
- new_moment_a: float32 [16, 16, 2048], P('groups', None, 'hid'), parts along dimension 0
- new_second_a: float32 [16, 16, 2048], P('groups', None, 'hid'), parts along dimension 0
- updated_output_maps: float32 [16, 16, 8192], P('groups', None, 'hid'), parts along dimension 0
- new_moment_b: float32 [16, 16, 8192], P('groups', None, 'hid'), parts along dimension 0
- new_second_b: float32 [16, 16, 8192], P('groups', None, 'hid'), parts along dimension 0
The draws below stay inside these ranges and needn't reach their ends.
There are 2 independent parts, one for each index of `groups`. The reference program is written for one: setup_inputs(seed, part) draws one part's arguments, and reference() takes and returns one part's arrays. A program takes and returns all parts, laid end to end along the dimension named above; an argument that names none is the same for every part. Nothing has to cross between parts.
Inputs may be any that keep to these rules, and one draw needn't show every extreme that they name: `active`: each row names 2 different hidden blocks; taking all entries of all rows, no hidden block is named more than 4 times, and some block exactly 4 times. Entries at positions counts[t] or later are padding.
All inputs are finite; a program needn't handle non-finite values.
Results may differ from the reference program's by a relative error of at most 0.0095.
Values may be sent and summed in bfloat16 or wider, within the bound.
No kernel may reach another device: no remote copies, remote signals or barrier semaphores. Data moves between devices by JAX's collectives and lax.ppermute only.
A program may use at most 192 MiB of HBM per device.

```python
import math
import jax
import jax.numpy as jnp
import numpy as np
from jax import lax

MODEL_WIDTH = 8192
BLOCK_EDGE = 128
ACTIVE_BLOCKS = 2
ADAPTER_RUNS = 8
ADAPTER_RANK = 16
NTILE = 4
HB = 16
HIDDEN_COUNT = 2048
TBLOCKS = 16
TOKENS = 2048
CAPR = 4


def draw_counts(key, part):
    key = jax.random.fold_in(key, 11)
    values = jax.random.randint(key, (TBLOCKS,), 1, ACTIVE_BLOCKS + 1)
    return values.at[0].set(ACTIVE_BLOCKS).astype(jnp.int32)


def draw_cotangent(key, part):
    key = jax.random.fold_in(key, 23)
    order_key, jitter_key, value_key = jax.random.split(key, 3)
    order = jax.random.permutation(order_key, ADAPTER_RUNS)
    jitter = jax.random.uniform(jitter_key, (ADAPTER_RUNS,), jnp.float32)
    level = (order.astype(jnp.float32) + jitter) / ADAPTER_RUNS
    run_scale = jnp.power(10.0, -3.0 + 3.0 * level)
    row_ids = jnp.arange(TOKENS, dtype=jnp.int32)
    row_run = row_ids // BLOCK_EDGE * ADAPTER_RUNS // TBLOCKS
    values = jnp.clip(jax.random.normal(value_key, (TOKENS, MODEL_WIDTH), jnp.float32), -5.0, 5.0)
    return (values * run_scale[row_run][:, None]).astype(jnp.bfloat16)


def set_ends(drawn, stream_key, smallest, top_value):
    place = [jax.random.randint(jax.random.fold_in(stream_key, axis), (), 0, length) for axis, length in enumerate(drawn.shape)]
    longest = drawn.shape.index(max(drawn.shape))
    neighbour = place[:longest] + [(place[longest] + 1) % drawn.shape[longest]] + place[longest + 1:]
    return drawn.at[tuple(place)].set(smallest).at[tuple(neighbour)].set(top_value)


def block_scale(own_key, dims, shards, least, top_value):
    loudness, own = 1.0, jax.random.fold_in(own_key, 6)
    for dim, parts in shards:
        heights = jnp.exp(jax.random.uniform(jax.random.fold_in(own, dim), (parts,), jnp.float32, least / len(shards), top_value / len(shards)))
        loudness = loudness * jnp.repeat(heights, dims[dim] // parts).reshape([-1 if axis == dim else 1 for axis in range(len(dims))])
    return loudness


def assign_block(key, own, number, rows, count, top, reach, skew):
    sequence = jax.random.permutation(key, count)
    crowded, usual = portions_of(count, rows * top, reach, skew, True), portions_of(count, rows * top, reach, skew, False)
    places = jnp.arange(count)

    def named(sizes, offset_by):
        used = int((sizes > 0).sum())
        fixed = max(1, used // 4)
        passed = fixed + (places - fixed + offset_by * (used - fixed)) % max(1, count - fixed)
        return jnp.zeros((count,), jnp.int32).at[sequence[jnp.where(places < fixed, places, passed)]].set(jnp.asarray(sizes, jnp.int32))

    sizes = jnp.where(number % 4 == 0, named(crowded, number // 4), named(usual, number - number // 4 - 1))
    mixed = jax.random.permutation(jax.random.fold_in(own, 3), count)
    source_of, receiver = mixed[0:count // 2 * 2:2], mixed[1:count // 2 * 2:2]
    room = jnp.minimum(sizes[source_of] - 1, reach - sizes[receiver]) // 2
    room = jnp.where((source_of == sequence[0]) | (receiver == sequence[0]) | (sizes[receiver] == 0), 0, jnp.maximum(room, 0))
    passed = jax.random.randint(jax.random.fold_in(own, 4), (count // 2,), 0, 1 << 20) % (room + 1)
    sizes = sizes.at[source_of].add(-passed).at[receiver].add(passed)
    members = jnp.searchsorted(jnp.cumsum(sizes), jnp.arange(rows * top), side="right").astype(jnp.int32)
    listing = members.reshape(top, rows).T
    listing = listing[jax.random.permutation(jax.random.fold_in(own, 1), rows)]
    offset_by = jax.random.randint(jax.random.fold_in(own, 2), (rows, 1), 0, top)
    return jnp.take_along_axis(listing, (jnp.arange(top)[None, :] + offset_by) % top, axis=1)


def portions_of(count, total, bound, skew, full):
    portions = [(1 << 20) // math.isqrt(grade ** skew) + 1 for grade in range(1, count + 1)]
    largest = bound if full else min(bound, max(-(-total // count), total * portions[0] // sum(portions)))
    least = 1 if total - largest >= count - 1 else 0
    holding, spare = [largest] + [least] * (count - 1), total - largest - least * (count - 1)
    while spare > 0:
        candidates = [i for i in range(1, count) if holding[i] < largest] or [i for i in range(1, count) if holding[i] < bound]
        mass, left = sum([portions[i] for i in candidates]), spare
        for i in candidates:
            addition = min(bound - holding[i], max(1, left * portions[i] // mass), spare)
            holding[i] = holding[i] + addition
            spare = spare - addition
    return np.array(holding)


def centred(rng, dims, scale, reach, cuts=(), kind=jnp.bfloat16):
    level = block_scale(rng, dims, cuts, -0.22, 0.18) if cuts else 1.0
    values = jax.random.normal(rng, dims, jnp.float32) * scale * level
    return jnp.minimum(jnp.maximum(values, -reach), reach).astype(kind)


def setup_inputs(seed: int = 0, part: int = 0) -> dict:
    keys = jax.random.split(jax.random.key(seed), 16)
    part_splits = jax.random.split(jax.random.fold_in(keys[15], part), 16)
    tokens = centred(part_splits[0], (TOKENS, MODEL_WIDTH), 1.0, 6.0, ((0, 16),))
    cotangent = draw_cotangent(jax.random.fold_in(jax.random.fold_in(keys[15], part), 71), part)
    gate_weight = centred(keys[2], (MODEL_WIDTH, HIDDEN_COUNT), MODEL_WIDTH ** -0.5, 0.0625, ((1, 16),))
    up_weight = centred(keys[3], (MODEL_WIDTH, HIDDEN_COUNT), MODEL_WIDTH ** -0.5, 0.0625, ((1, 16),))
    down_weight = centred(keys[4], (HIDDEN_COUNT, MODEL_WIDTH), (BLOCK_EDGE * ACTIVE_BLOCKS) ** -0.5, 0.375, ((0, 16),))
    adapter_input_maps = centred(part_splits[5], (ADAPTER_RUNS, ADAPTER_RANK, HIDDEN_COUNT), (BLOCK_EDGE * ACTIVE_BLOCKS) ** -0.5, 0.375, ((2, 16),), jnp.float32)
    adapter_output_maps = centred(part_splits[6], (ADAPTER_RUNS, ADAPTER_RANK, MODEL_WIDTH), ADAPTER_RANK ** -0.5, 1.5, ((2, 16),), jnp.float32)
    first_moment_input = centred(part_splits[7], (ADAPTER_RUNS, ADAPTER_RANK, HIDDEN_COUNT), 1.0, 6.0, ((2, 16),), jnp.float32)
    second_moment_input = jnp.clip(jnp.exp(math.log(2.0) - 2.9957323 * jax.random.uniform(part_splits[8], (ADAPTER_RUNS, ADAPTER_RANK, HIDDEN_COUNT), jnp.float32) ** block_scale(part_splits[8], (ADAPTER_RUNS, ADAPTER_RANK, HIDDEN_COUNT), ((2, 16),), -0.2, 0.2)), 0.1, 2.0)
    first_moment_output = centred(part_splits[9], (ADAPTER_RUNS, ADAPTER_RANK, MODEL_WIDTH), 1.0, 6.0, ((2, 16),), jnp.float32)
    second_moment_output = jnp.clip(jnp.exp(math.log(2.0) - 2.9957323 * jax.random.uniform(part_splits[10], (ADAPTER_RUNS, ADAPTER_RANK, MODEL_WIDTH), jnp.float32) ** block_scale(part_splits[10], (ADAPTER_RUNS, ADAPTER_RANK, MODEL_WIDTH), ((2, 16),), -0.2, 0.2)), 0.1, 2.0)
    active_keys = jax.random.split(jax.random.fold_in(part_splits[11], 1), TBLOCKS // TBLOCKS)
    active_turns = jax.random.permutation(jax.random.fold_in(part_splits[11], 3), TBLOCKS // TBLOCKS)
    active = jax.vmap(lambda own, number: assign_block(jax.random.fold_in(part_splits[11], 2), own, number, TBLOCKS, HB, ACTIVE_BLOCKS, CAPR, 2))(active_keys, active_turns).reshape((TBLOCKS, ACTIVE_BLOCKS))
    counts = draw_counts(jax.random.fold_in(jax.random.fold_in(keys[15], part), 71), part)
    dropout_tiles = set_ends((jax.random.randint(keys[13], (NTILE, BLOCK_EDGE, BLOCK_EDGE), 0, 10) < 9).astype(jnp.int32), jax.random.fold_in(keys[13], 1), 0, 1)
    seeds = set_ends(jax.random.randint(part_splits[14], (ADAPTER_RUNS,), 0, NTILE), jax.random.fold_in(part_splits[14], 1), 0, NTILE - 1).astype(jnp.int32)
    return {"tokens": tokens, "cotangent": cotangent, "gate_weight": gate_weight, "up_weight": up_weight, "down_weight": down_weight, "adapter_input_maps": adapter_input_maps, "adapter_output_maps": adapter_output_maps, "first_moment_input": first_moment_input, "second_moment_input": second_moment_input, "first_moment_output": first_moment_output, "second_moment_output": second_moment_output, "active": active, "counts": counts, "dropout_tiles": dropout_tiles, "seeds": seeds}


adapter_scale = 2.0 / 0.9

def adamw_step_update(param, moment, second, grad):
    moment_next = 0.9 * moment + 0.1 * grad
    second_next = 0.999 * second + 0.001 * grad * grad
    corrected = moment_next / (1.0 - 0.9 ** 10)
    spread = jnp.sqrt(second_next / (1.0 - 0.999 ** 10)) + 1e-08
    return (param - 0.01 * (corrected / spread + 0.1 * param), moment_next, second_next)

def reference(tokens, cotangent, gate_weight, up_weight, down_weight, adapter_input_maps, adapter_output_maps, first_moment_input, second_moment_input, first_moment_output, second_moment_output, active, counts, dropout_tiles, seeds):
    adapter_in_half = adapter_input_maps.astype(jnp.bfloat16)
    adapter_out_half = adapter_output_maps.astype(jnp.bfloat16)

    def step(carry, index):
        input_map_gradient, output_map_gradient = carry
        rows = lax.dynamic_slice_in_dim(tokens, index * BLOCK_EDGE, BLOCK_EDGE, 0)
        gradient_rows = lax.dynamic_slice_in_dim(cotangent, index * BLOCK_EDGE, BLOCK_EDGE, 0)
        run_index = (index * ADAPTER_RUNS // TBLOCKS).astype(jnp.int32)
        block_run_index = adapter_out_half[run_index]
        base_output = jnp.zeros((BLOCK_EDGE, MODEL_WIDTH), jnp.float32)
        low_sum = jnp.zeros((BLOCK_EDGE, ADAPTER_RANK), jnp.float32)
        kept = []
        for slot in range(ACTIVE_BLOCKS):
            block = active[index, slot].astype(jnp.int32)
            valid = (slot < counts[index]).astype(jnp.float32)
            start = (block * BLOCK_EDGE).astype(jnp.int32)
            gate = jnp.dot(rows, lax.dynamic_slice_in_dim(gate_weight, start, BLOCK_EDGE, 1), preferred_element_type=jnp.float32)
            upper = jnp.dot(rows, lax.dynamic_slice_in_dim(up_weight, start, BLOCK_EDGE, 1), preferred_element_type=jnp.float32)
            hidden = (jax.nn.silu(gate) * upper).astype(jnp.bfloat16)
            partial_value = jnp.dot(hidden, lax.dynamic_slice_in_dim(down_weight, start, BLOCK_EDGE, 0), preferred_element_type=jnp.float32).astype(jnp.bfloat16)
            base_output = base_output + partial_value.astype(jnp.float32) * valid
            tile_index = ((seeds[run_index] + index + 3 * block) % NTILE).astype(jnp.int32)
            dropped = hidden * dropout_tiles[tile_index].astype(jnp.bfloat16)
            a_block = lax.dynamic_slice(adapter_in_half, (run_index, jnp.int32(0), start), (1, ADAPTER_RANK, BLOCK_EDGE))[0]
            low = jnp.dot(dropped, a_block.T, preferred_element_type=jnp.float32).astype(jnp.bfloat16)
            low_sum = low_sum + low.astype(jnp.float32) * valid
            kept.append((start, dropped, valid))
        base_block_output = base_output.astype(jnp.bfloat16)
        low_rank_block = low_sum.astype(jnp.bfloat16)
        adapter_extra = jnp.dot(low_rank_block, block_run_index, preferred_element_type=jnp.float32)
        layer_result = (base_block_output.astype(jnp.float32) + adapter_scale * adapter_extra).astype(jnp.bfloat16)
        low_rank_gradient = (adapter_scale * jnp.dot(gradient_rows, block_run_index.T, preferred_element_type=jnp.float32)).astype(jnp.bfloat16)
        output_map_gradient = output_map_gradient.at[run_index].add(adapter_scale * jnp.dot(low_rank_block.T, gradient_rows, preferred_element_type=jnp.float32))
        for start, dropped, valid in kept:
            contrib = jnp.dot(low_rank_gradient.T, dropped, preferred_element_type=jnp.float32) * valid
            old = lax.dynamic_slice(input_map_gradient, (run_index, jnp.int32(0), start), (1, ADAPTER_RANK, BLOCK_EDGE))
            input_map_gradient = lax.dynamic_update_slice(input_map_gradient, old + contrib[None], (run_index, jnp.int32(0), start))
        return ((input_map_gradient, output_map_gradient), layer_result)
    init = (jnp.zeros((ADAPTER_RUNS, ADAPTER_RANK, HIDDEN_COUNT), jnp.float32), jnp.zeros((ADAPTER_RUNS, ADAPTER_RANK, MODEL_WIDTH), jnp.float32))
    (input_map_gradient, output_map_gradient), outputs = lax.scan(step, init, jnp.arange(TBLOCKS, dtype=jnp.int32))
    output = outputs.reshape(TBLOCKS * BLOCK_EDGE, MODEL_WIDTH)
    norm_sq = lax.optimization_barrier(jnp.sum(input_map_gradient * input_map_gradient, axis=(1, 2))) + lax.optimization_barrier(jnp.sum(output_map_gradient * output_map_gradient, axis=(1, 2)))
    limit = math.sqrt(ADAPTER_RANK * (HIDDEN_COUNT + MODEL_WIDTH))
    clip_factor = jnp.minimum(1.0, limit / jnp.sqrt(norm_sq))
    updated_input_maps, next_first_input, next_second_input = adamw_step_update(adapter_input_maps, first_moment_input, second_moment_input, input_map_gradient * clip_factor[:, None, None])
    updated_output_maps, next_first_output, next_second_output = adamw_step_update(adapter_output_maps, first_moment_output, second_moment_output, output_map_gradient * clip_factor[:, None, None])
    return (output, updated_input_maps, next_first_input, next_second_input, updated_output_maps, next_first_output, next_second_output)
```

```python
import functools
import math

import jax
import jax.numpy as jnp
from jax import lax
from jax.experimental import pallas as pl
from jax.experimental.pallas import tpu as pltpu
from jax.sharding import Mesh, PartitionSpec as P

adapter_scale = 2.0 / 0.9
bf16 = jnp.bfloat16
f32 = jnp.float32
vmem_limit = 48 * 1024 * 1024


def dot(a, b, dims=((1,), (0,))):
    return lax.dot_general(a, b, (dims, ((), ())), preferred_element_type=f32)


def adamw_step_update(param, moment, second, grad):
    moment_next = 0.9 * moment + 0.1 * grad
    second_next = 0.999 * second + 0.001 * grad * grad
    corrected = moment_next / (1.0 - 0.9**10)
    spread = jnp.sqrt(second_next / (1.0 - 0.999**10)) + 1e-08
    return (param - 0.01 * (corrected / spread + 0.1 * param), moment_next, second_next)


def partial_kernel(tok, active, x_ref, wm_ref, wo_ref, o_ref, *, block, chunk, picks):
    t = tok[pl.program_id(0)]
    x = x_ref[0, :block, :]
    for k in range(picks):
        j = active[t, k]
        o_ref[0, k, :, :block] = dot(x, wm_ref[j, :chunk, :]).astype(o_ref.dtype)
        o_ref[0, k, :, block:] = dot(x, wo_ref[j, :chunk, :]).astype(o_ref.dtype)


def partial_products(tok, active, xb, wm, wo, block, chunk):
    picks = active.shape[1]
    steps = tok.shape[0]
    whole = lambda a: pl.BlockSpec(a.shape, lambda i, *_: (0, 0, 0))
    return pl.pallas_call(
        functools.partial(partial_kernel, block=block, chunk=chunk, picks=picks),
        out_shape=jax.ShapeDtypeStruct((steps, picks, block, 2 * block), bf16),
        grid_spec=pltpu.PrefetchScalarGridSpec(
            num_scalar_prefetch=2,
            grid=(steps,),
            in_specs=[
                pl.BlockSpec((1,) + xb.shape[1:], lambda i, tok, act: (tok[i], 0, 0)),
                whole(wm),
                whole(wo),
            ],
            out_specs=pl.BlockSpec((1, picks, block, 2 * block), lambda i, *_: (i, 0, 0, 0)),
        ),
        compiler_params=pltpu.CompilerParams(vmem_limit_bytes=vmem_limit),
        cost_estimate=pl.CostEstimate(
            flops=steps * picks * 4 * block * block * chunk,
            bytes_accessed=2 * (wm.size + wo.size + xb.size // 2 + steps * picks * 2 * block * block),
            transcendentals=0,
        ),
        name="gate_up_partial",
    )(tok, active, xb, wm, wo)


def hidden_kernel(flags, r_ref, tile_ref, a_ref, dzt_ref, o_ref, *, block, picks, rank):
    total = jnp.sum(r_ref[...].astype(f32), axis=0)
    swap = flags[0] == 1
    low_t = jnp.zeros((rank, block), f32)
    for k in range(picks):
        first, second = total[k, :, :block], total[k, :, block:]
        gate = jnp.where(swap, second, first)
        up = jnp.where(swap, first, second)
        hidden = (gate / (1.0 + jnp.exp(-gate)) * up).astype(bf16)
        hidden = jnp.where(flags[1 + k] == 1, hidden, jnp.zeros_like(hidden))
        dropped = hidden * tile_ref[flags[1 + picks + k]].astype(f32).astype(bf16)
        low_t += dot(a_ref[k], dropped, ((1,), (1,))).astype(bf16).astype(f32)
        o_ref[k * block : (k + 1) * block, :] = hidden
        base = picks * block + rank * (1 + k)
        o_ref[base : base + rank, :] = dot(dzt_ref[...], dropped).astype(bf16)
    o_ref[picks * block : picks * block + rank, :] = low_t.astype(bf16)


def output_kernel(pos, active, h_ref, d_ref, b_ref, o_ref, *, block, picks, rank, per, runs, n):
    for s in range(per):
        t = pl.program_id(0) * per + s
        p = pos[t]
        acc = None
        for k in range(picks):
            j = active[t, k]
            part = dot(h_ref[p, k * block : (k + 1) * block, :], d_ref[j]).astype(bf16).astype(f32)
            acc = part if acc is None else acc + part
        base = acc.astype(bf16).astype(f32)
        z_t = h_ref[p, picks * block : picks * block + rank, :]
        extra = dot(z_t, b_ref[t * runs // n], ((0,), (0,)))
        o_ref[s] = (base + adapter_scale * extra).astype(bf16)


def body(
    tokens,
    cotangent,
    gate_weight,
    up_weight,
    down_weight,
    adapter_input_maps,
    adapter_output_maps,
    first_moment_input,
    second_moment_input,
    first_moment_output,
    second_moment_output,
    active,
    counts,
    dropout_tiles,
    seeds,
):
    hid = ("chip", "core")
    chips, cores = lax.axis_size("chip"), lax.axis_size("core")
    n = chips * cores
    group, core = lax.axis_index("groups"), lax.axis_index("core")
    me = lax.axis_index("chip") * cores + core
    model = tokens.shape[1]
    tiles_n, block = dropout_tiles.shape[0], dropout_tiles.shape[1]
    picks = active.shape[1]
    runs, rank = adapter_output_maps.shape[0], adapter_output_maps.shape[1]
    chunk = model // n
    half = chunk // 2
    blocks = jnp.arange(n, dtype=jnp.int32)
    run_of = blocks * runs // n
    my_run = me * runs // n
    mine = lax.dynamic_index_in_dim(active, me, 0, keepdims=False)
    my_count = lax.dynamic_index_in_dim(counts, me, 0, keepdims=False)
    a_bf = adapter_input_maps.astype(bf16)
    b_bf = adapter_output_maps.astype(bf16)
    per_run = n // runs

    w_rows = jnp.where(group == 0, gate_weight, up_weight).reshape(n, chunk, block)
    w_send = jnp.concatenate([w_rows, jnp.repeat(a_bf, per_run, axis=0)], axis=1)
    wm = lax.all_to_all(w_send, hid, split_axis=0, concat_axis=0, tiled=True)
    other = [(0, 1), (1, 0)]
    wo = lax.ppermute(wm, "groups", other)

    x_rows = jnp.transpose(tokens.reshape(block, n, chunk), (1, 0, 2))
    x_send = jnp.concatenate([x_rows, jnp.repeat(b_bf, per_run, axis=0)], axis=1)
    xb = lax.all_to_all(x_send, hid, split_axis=0, concat_axis=0, tiled=True)

    d_cols = jnp.transpose(down_weight.reshape(block, n, 2, half), (1, 2, 0, 3))
    d_send = lax.dynamic_index_in_dim(d_cols, group, 1, keepdims=False)
    dm = lax.all_to_all(d_send, hid, split_axis=0, concat_axis=0, tiled=True)
    do = lax.ppermute(dm, "groups", other)
    d_all = jnp.where(
        group == 0, jnp.concatenate([dm, do], axis=2), jnp.concatenate([do, dm], axis=2)
    )

    my_b = jnp.transpose(xb[:, block:, :], (1, 0, 2)).reshape(rank, model)
    dz_t = (adapter_scale * dot(my_b, cotangent, ((1,), (1,)))).astype(bf16)
    my_a = wm[mine, chunk:, :]

    evens = jnp.arange(chips, dtype=jnp.int32) * cores
    sent = partial_products(evens + (1 - core), active, xb, wm, wo, block, chunk)
    got = lax.ppermute(sent, "core", other)
    kept = partial_products(evens + core, active, xb, wm, wo, block, chunk)
    paired = (kept.astype(f32) + got.astype(f32)).astype(bf16)
    summed = lax.all_to_all(paired, "chip", split_axis=0, concat_axis=0, tiled=True)

    tile_pick = (seeds[my_run] + me + 3 * mine) % tiles_n
    flags = jnp.concatenate(
        [
            group[None].astype(jnp.int32),
            (jnp.arange(picks) < my_count).astype(jnp.int32),
            tile_pick.astype(jnp.int32),
        ]
    )
    rows = picks * block + rank * (1 + picks)
    vmem = pl.BlockSpec(memory_space=pltpu.VMEM)
    held = pl.pallas_call(
        functools.partial(hidden_kernel, block=block, picks=picks, rank=rank),
        out_shape=jax.ShapeDtypeStruct((rows, block), bf16),
        in_specs=[pl.BlockSpec(memory_space=pltpu.SMEM), vmem, vmem, vmem, vmem],
        out_specs=vmem,
        compiler_params=pltpu.CompilerParams(vmem_limit_bytes=vmem_limit),
        name="hidden_values",
    )(flags, summed, dropout_tiles, my_a, dz_t)

    z_t = held[picks * block : picks * block + rank]
    term_b = adapter_scale * dot(z_t, cotangent)
    term_b = jnp.transpose(term_b.reshape(rank, n, chunk), (1, 0, 2))
    parts_b = lax.all_to_all(term_b, hid, split_axis=0, concat_axis=0, tiled=True)
    grad_b = jnp.sum(parts_b.reshape(runs, per_run, rank, chunk), axis=1)

    gathered = held[None]
    where = blocks[:1]
    mask = chips // 2
    while mask:
        swapped = lax.ppermute(gathered, "chip", [(i, i ^ mask) for i in range(chips)])
        gathered = jnp.concatenate([gathered, swapped], axis=0)
        where = jnp.concatenate([where, where ^ (mask * cores)])
        mask //= 2
    swapped = lax.ppermute(gathered, "core", other)
    gathered = jnp.concatenate([gathered, swapped], axis=0)
    where = jnp.concatenate([where, where ^ 1]) ^ me
    pos = jnp.zeros((n,), jnp.int32).at[where].set(blocks)

    per = 4
    out_chunks = pl.pallas_call(
        functools.partial(
            output_kernel, block=block, picks=picks, rank=rank, per=per, runs=runs, n=n
        ),
        out_shape=jax.ShapeDtypeStruct((n, block, chunk), bf16),
        grid_spec=pltpu.PrefetchScalarGridSpec(
            num_scalar_prefetch=2,
            grid=(n // per,),
            in_specs=[
                pl.BlockSpec(gathered.shape, lambda i, *_: (0, 0, 0)),
                pl.BlockSpec(d_all.shape, lambda i, *_: (0, 0, 0)),
                pl.BlockSpec(b_bf.shape, lambda i, *_: (0, 0, 0)),
            ],
            out_specs=pl.BlockSpec((per, block, chunk), lambda i, *_: (i, 0, 0)),
        ),
        compiler_params=pltpu.CompilerParams(vmem_limit_bytes=vmem_limit),
        name="output_columns",
    )(pos, active, gathered, d_all, b_bf)
    out_cols = lax.all_to_all(out_chunks, hid, split_axis=0, concat_axis=0, tiled=True)
    output = jnp.transpose(out_cols, (1, 0, 2)).reshape(block, model)

    terms_a = gathered[:, picks * block + rank :, :].reshape(n * picks, rank * block)
    run_at = (where * runs // n)[:, None]
    named = (active[where] == me) & (jnp.arange(picks)[None, :] < counts[where][:, None])
    hot = (run_at[None] == jnp.arange(runs)[:, None, None]) & named[None]
    grad_a = dot(hot.reshape(runs, n * picks).astype(bf16), terms_a).reshape(runs, rank, block)

    squares = jnp.sum(grad_a * grad_a, axis=(1, 2)) + jnp.sum(grad_b * grad_b, axis=(1, 2))
    totals = jnp.sum(lax.all_gather(squares, hid, axis=0), axis=0)
    limit = math.sqrt(rank * (n * block + model))
    factor = jnp.minimum(1.0, limit / jnp.sqrt(totals))[:, None, None]
    new_a = adamw_step_update(
        adapter_input_maps, first_moment_input, second_moment_input, grad_a * factor
    )
    new_b = adamw_step_update(
        adapter_output_maps, first_moment_output, second_moment_output, grad_b * factor
    )
    return (output, *new_a, *new_b)


def solution(mesh):
    groups, n = mesh.devices.shape
    fine = Mesh(mesh.devices.reshape(groups, n // 2, 2), ("groups", "chip", "core"))
    hid = ("chip", "core")
    rows = P(("groups",) + hid, None)
    maps = P("groups", None, hid)
    return jax.shard_map(
        body,
        mesh=fine,
        in_specs=(rows, rows, P(None, hid), P(None, hid), P(hid, None))
        + (maps,) * 6
        + (P("groups", None), P("groups"), P(), P("groups")),
        out_specs=(rows,) + (maps,) * 6,
        check_vma=False,
    )
```

```python
import functools
import math

import jax
import jax.numpy as jnp
from jax import lax
from jax.experimental import pallas as pl
from jax.experimental.pallas import tpu as pltpu
from jax.sharding import Mesh, PartitionSpec as P

adapter_scale = 2.0 / 0.9
bf16 = jnp.bfloat16
f32 = jnp.float32
vmem_limit = 48 * 1024 * 1024
vmem_full = 62 * 1024 * 1024
strips = 8
paired_step = 4


def dot(a, b, dims=((1,), (0,))):
    return lax.dot_general(a, b, (dims, ((), ())), preferred_element_type=f32)


def call(kernel, name, out, grid, in_specs, out_specs, scalars, arrays, flops=0):
    outs = out if isinstance(out, (tuple, list)) else [out]
    moved = sum(a.size * a.dtype.itemsize for a in (*arrays, *outs))
    return pl.pallas_call(
        kernel,
        out_shape=out,
        grid_spec=pltpu.PrefetchScalarGridSpec(
            num_scalar_prefetch=len(scalars),
            grid=grid,
            in_specs=in_specs,
            out_specs=out_specs,
        ),
        compiler_params=pltpu.CompilerParams(vmem_limit_bytes=vmem_limit),
        cost_estimate=pl.CostEstimate(flops=flops, bytes_accessed=moved, transcendentals=0),
        name=name,
    )(*scalars, *arrays)


def whole(a):
    zeros = (0,) * len(a.shape)
    return pl.BlockSpec(a.shape, lambda i, *_: zeros)


def weight_rows_kernel(gate_ref, up_ref, a_ref, o_ref, held, loads, stores, *, chunk, n, runs):
    group = lax.axis_index("groups")

    def copies(w_ref):
        return [
            pltpu.make_async_copy(
                w_ref.at[pl.ds(s * chunk, chunk)], held.at[s, pl.ds(0, chunk)], loads.at[s]
            )
            for s in range(n)
        ]

    @pl.when(group == 0)
    def _():
        for copy in copies(gate_ref):
            copy.start()

    @pl.when(group != 0)
    def _():
        for copy in copies(up_ref):
            copy.start()

    for s in range(n):
        held[s, chunk:, :] = a_ref[s * runs // n].astype(bf16)
    out = [pltpu.make_async_copy(held.at[s], o_ref.at[s], stores.at[s]) for s in range(n)]
    for s, copy in enumerate(copies(gate_ref)):
        copy.wait()
        out[s].start()
    for copy in out:
        copy.wait()


def token_columns_kernel(ids, x_ref, b_ref, o_ref, *, block, chunk, n, runs):
    per = n // strips
    for s in range(per):
        o_ref[s, :block, :] = x_ref[:, s * chunk : (s + 1) * chunk]
        run = (pl.program_id(0) * per + s) * runs // n
        o_ref[s, block:, :] = b_ref[run].astype(bf16)


def down_columns_kernel(ids, d_ref, o_ref, *, chunk, n):
    half = chunk // 2
    for s in range(n // strips):
        base = s * chunk

        @pl.when(ids[0] == 0)
        def _():
            o_ref[s] = d_ref[:, base : base + half]

        @pl.when(ids[0] != 0)
        def _():
            o_ref[s] = d_ref[:, base + half : base + chunk]


def partial_kernel(ids, active, x_ref, wm_ref, wo_ref, o_ref, *, block, chunk, picks, away):
    side = jnp.bitwise_xor(ids[1], away)
    for s in range(paired_step):
        x = x_ref[s, 0, :block, :]
        for k in range(picks):
            j = active[2 * (paired_step * pl.program_id(0) + s) + side, k]
            w = jnp.concatenate([wm_ref[j, :chunk, :], wo_ref[j, :chunk, :]], axis=1)
            o_ref[s, k] = dot(x, w).astype(o_ref.dtype)


def partial_products(ids, active, xb, wm, wo, block, chunk, away):
    n, picks = active.shape
    shape = (n // 2, picks, block, 2 * block)
    token = lambda i, ids, act: (i, jnp.bitwise_xor(ids[1], away), 0, 0)
    xp = xb.reshape(n // 2, 2, *xb.shape[1:])
    return call(
        functools.partial(partial_kernel, block=block, chunk=chunk, picks=picks, away=away),
        "gate_up_partial",
        jax.ShapeDtypeStruct(shape, bf16),
        (n // 2 // paired_step,),
        [pl.BlockSpec((paired_step, 1) + xb.shape[1:], token), whole(wm), whole(wo)],
        pl.BlockSpec((paired_step,) + shape[1:], lambda i, *_: (i, 0, 0, 0)),
        (ids, active),
        (xp, wm, wo),
        flops=n * picks * 2 * block * block * chunk,
    )


def side_rows_kernel(ids, active, counts, seeds, *refs, block, chunk, picks, rank, n):
    b_ref, dy_ref = refs[:2]
    tile_refs, a_refs, o_ref = refs[2 : 2 + picks], refs[2 + picks : -1], refs[-1]
    total = None
    for e in range(n):
        part = dot(b_ref[e], dy_ref[:, e * chunk : (e + 1) * chunk], ((1,), (1,)))
        total = part if total is None else total + part
    for k in range(picks):
        o_ref[k * block : (k + 1) * block, :] = tile_refs[k][0].astype(f32).astype(bf16)
        base = picks * block + rank * (1 + k)
        o_ref[base : base + rank, :] = a_refs[k][0]
    base = picks * block
    o_ref[base : base + rank, :] = (adapter_scale * total).astype(bf16)


def hidden_kernel(ids, counts, r_ref, side_ref, o_ref, *, block, picks, rank):
    total = jnp.sum(r_ref[...].astype(f32), axis=0)
    swap = ids[0] != 0
    count = counts[ids[2]]
    low_t = jnp.zeros((rank, block), f32)
    own = slice(picks * block, picks * block + rank)
    for k in range(picks):
        first, second = total[k, :, :block], total[k, :, block:]
        gate = jnp.where(swap, second, first)
        up = jnp.where(swap, first, second)
        hidden = (gate / (1.0 + jnp.exp(-gate)) * up).astype(bf16)
        hidden = jnp.where(k < count, hidden, jnp.zeros_like(hidden))
        rows = slice(k * block, (k + 1) * block)
        pair = slice(picks * block + rank * (1 + k), picks * block + rank * (2 + k))
        dropped = hidden * side_ref[rows, :]
        low_t += dot(side_ref[pair, :], dropped, ((1,), (1,))).astype(bf16).astype(f32)
        o_ref[rows, :] = hidden
        o_ref[pair, :] = dot(side_ref[own, :], dropped).astype(bf16)
    o_ref[own, :] = low_t.astype(bf16)


def output_terms_kernel(ids, z_ref, dy_ref, o_ref, *, chunk, n):
    for s in range(n // strips):
        part = dot(z_ref[...], dy_ref[:, s * chunk : (s + 1) * chunk])
        o_ref[s] = (adapter_scale * part).astype(bf16)


def output_kernel(
    ids, active, slot, h_ref, dm_ref, do_ref, b_ref, o_ref, *, block, picks, rank, per, runs, n
):
    half = dm_ref.shape[2]
    swap = ids[0] != 0
    for s in range(per):
        t = pl.program_id(0) * per + s
        p = slot[jnp.bitwise_xor(t, ids[2])]
        sums = [None, None]
        for k in range(picks):
            j = active[t, k]
            h = h_ref[p, k * block : (k + 1) * block, :]
            for side, d_ref in enumerate((dm_ref, do_ref)):
                part = dot(h, d_ref[j]).astype(bf16).astype(f32)
                sums[side] = part if k == 0 else sums[side] + part
        left = jnp.where(swap, sums[1], sums[0]).astype(bf16).astype(f32)
        right = jnp.where(swap, sums[0], sums[1]).astype(bf16).astype(f32)
        z_t = h_ref[p, picks * block : picks * block + rank, :]
        extra = adapter_scale * dot(z_t, b_ref[t * runs // n].astype(bf16), ((0,), (0,)))
        o_ref[s, :, :half] = (left + extra[:, :half]).astype(bf16)
        o_ref[s, :, half:] = (right + extra[:, half:]).astype(bf16)


def join_columns_kernel(ids, c_ref, o_ref, *, chunk, n):
    for s in range(n // strips):
        o_ref[:, s * chunk : (s + 1) * chunk] = c_ref[s]


def join_copies_kernel(c_ref, o_ref, held, loads, stores, *, chunk, n):
    into = [pltpu.make_async_copy(c_ref.at[s], held.at[s], loads.at[s]) for s in range(n)]
    out = [
        pltpu.make_async_copy(held.at[s], o_ref.at[:, pl.ds(s * chunk, chunk)], stores.at[s])
        for s in range(n)
    ]
    for copy in into:
        copy.start()
    for first, second in zip(into, out):
        first.wait()
        second.start()
    for copy in out:
        copy.wait()


def gradients_kernel(ids, active, counts, order, *refs, picks, runs, n):
    term_refs, part_ref, ga_ref, gb_ref, sq_ref = refs[:picks], *refs[picks:]
    me = ids[2]
    per_run = n // runs
    ga_ref[...] = jnp.zeros_like(ga_ref)

    def add(s, carry):
        t = jnp.bitwise_xor(order[s], me)
        for k in range(picks):

            @pl.when((active[t, k] == me) & (k < counts[t]))
            def _():
                run = t * runs // n
                ga_ref[run] = ga_ref[run] + term_refs[k][s].astype(f32)

        return carry

    lax.fori_loop(0, n, add, 0)
    for r in range(runs):
        total = part_ref[r * per_run].astype(f32)
        for q in range(1, per_run):
            total = total + part_ref[r * per_run + q].astype(f32)
        gb_ref[r] = total
        square = jnp.sum(ga_ref[r] * ga_ref[r]) + jnp.sum(total * total)
        sq_ref[r : r + 1, :] = jnp.full((1, sq_ref.shape[1]), square, f32)


def adamw_kernel(ids, sq_ref, *refs, limit, runs):
    ins, outs = refs[:8], refs[8:]
    for r in range(runs):
        factor = jnp.minimum(1.0, limit / jnp.sqrt(sq_ref[r : r + 1, :1]))
        for side in range(2):
            p_ref, m_ref, v_ref, g_ref = ins[4 * side : 4 * side + 4]
            grad = g_ref[r] * factor
            param = p_ref[r]
            moment = 0.9 * m_ref[r] + 0.1 * grad
            second = 0.999 * v_ref[r] + 0.001 * grad * grad
            corrected = moment / (1.0 - 0.9**10)
            spread = jnp.sqrt(second / (1.0 - 0.999**10)) + 1e-08
            outs[3 * side][r] = param - 0.01 * (corrected / spread + 0.1 * param)
            outs[3 * side + 1][r] = moment
            outs[3 * side + 2][r] = second


def body(
    tokens,
    cotangent,
    gate_weight,
    up_weight,
    down_weight,
    adapter_input_maps,
    adapter_output_maps,
    first_moment_input,
    second_moment_input,
    first_moment_output,
    second_moment_output,
    active,
    counts,
    dropout_tiles,
    seeds,
):
    hid = ("chip", "core")
    chips, cores = lax.axis_size("chip"), lax.axis_size("core")
    n = chips * cores
    core = lax.axis_index("core")
    me = lax.axis_index("chip") * cores + core
    ids = jnp.stack([lax.axis_index("groups"), core, me]).astype(jnp.int32)
    model = tokens.shape[1]
    tiles_n, block = dropout_tiles.shape[0], dropout_tiles.shape[1]
    picks = active.shape[1]
    runs, rank = adapter_output_maps.shape[0], adapter_output_maps.shape[1]
    chunk = model // n
    half = chunk // 2
    per = n // strips
    strip = model // strips
    other = [(0, 1), (1, 0)]
    across = lambda m: [(i, i ^ m) for i in range(chips)]
    sizes = dict(chunk=chunk, n=n)

    anywhere = pl.BlockSpec(memory_space=pl.ANY)
    w_send = pl.pallas_call(
        functools.partial(weight_rows_kernel, runs=runs, **sizes),
        out_shape=jax.ShapeDtypeStruct((n, chunk + rank, block), bf16),
        in_specs=[anywhere, anywhere, pl.BlockSpec(memory_space=pltpu.VMEM)],
        out_specs=anywhere,
        scratch_shapes=[
            pltpu.VMEM((n, chunk + rank, block), bf16),
            pltpu.SemaphoreType.DMA((n,)),
            pltpu.SemaphoreType.DMA((n,)),
        ],
        compiler_params=pltpu.CompilerParams(vmem_limit_bytes=vmem_full),
        name="weight_rows",
    )(gate_weight, up_weight, adapter_input_maps)
    wm = lax.all_to_all(w_send, hid, split_axis=0, concat_axis=0, tiled=True)
    wo = lax.ppermute(wm, "groups", other)

    x_send = call(
        functools.partial(token_columns_kernel, block=block, runs=runs, **sizes),
        "token_columns",
        jax.ShapeDtypeStruct((n, block + rank, chunk), bf16),
        (strips,),
        [pl.BlockSpec((block, strip), lambda i, ids: (0, i)), whole(adapter_output_maps)],
        pl.BlockSpec((per, block + rank, chunk), lambda i, ids: (i, 0, 0)),
        (ids,),
        (tokens, adapter_output_maps),
    )
    xb = lax.all_to_all(x_send, hid, split_axis=0, concat_axis=0, tiled=True)

    d_send = call(
        functools.partial(down_columns_kernel, **sizes),
        "down_columns",
        jax.ShapeDtypeStruct((n, block, half), bf16),
        (strips,),
        [pl.BlockSpec((block, strip), lambda i, ids: (0, i))],
        pl.BlockSpec((per, block, half), lambda i, ids: (i, 0, 0)),
        (ids,),
        (down_weight,),
    )
    d_send, xb = lax.optimization_barrier((d_send, xb))
    dm = lax.all_to_all(d_send, hid, split_axis=0, concat_axis=0, tiled=True)

    sent = partial_products(ids, active, xb, wm, wo, block, chunk, 1)
    got = lax.ppermute(sent, "core", other)
    kept = partial_products(ids, active, xb, wm, wo, block, chunk, 0)
    paired = (kept.astype(f32) + got.astype(f32)).astype(bf16)
    paired, dm = lax.optimization_barrier((paired, dm))
    summed = lax.all_to_all(paired, "chip", split_axis=0, concat_axis=0, tiled=True)

    do = lax.ppermute(dm, "groups", other)

    rows = picks * block + rank * (1 + picks)

    def tile_spec(k):
        def at(i, ids, active, counts, seeds):
            me = ids[2]
            pick = seeds[me * runs // n] + me + 3 * active[me, k]
            return (lax.rem(pick, tiles_n), 0, 0)

        return pl.BlockSpec((1, block, block), at)

    def map_spec(k):
        return pl.BlockSpec(
            (1, rank, block), lambda i, ids, active, *_: (active[ids[2], k], chunk // rank, 0)
        )

    side = call(
        functools.partial(side_rows_kernel, block=block, picks=picks, rank=rank, **sizes),
        "side_rows",
        jax.ShapeDtypeStruct((rows, block), bf16),
        (1,),
        [pl.BlockSpec((n, rank, chunk), lambda i, *_: (0, block // rank, 0)), whole(cotangent)]
        + [tile_spec(k) for k in range(picks)]
        + [map_spec(k) for k in range(picks)],
        pl.BlockSpec((rows, block), lambda i, *_: (0, 0)),
        (ids, active, counts, seeds),
        (xb, cotangent) + (dropout_tiles,) * picks + (wm,) * picks,
    )
    held = call(
        functools.partial(hidden_kernel, block=block, picks=picks, rank=rank),
        "hidden_values",
        jax.ShapeDtypeStruct((rows, block), bf16),
        (1,),
        [whole(summed), whole(side)],
        pl.BlockSpec((rows, block), lambda i, *_: (0, 0)),
        (ids, counts),
        (summed, side),
    )

    far, near = chips // 2, chips // 4
    order = [0, far * cores, near * cores, (far + near) * cores]
    gathered = jnp.stack(
        [held] + [lax.ppermute(held, "chip", across(m)) for m in (far, near, far + near)]
    )
    mask = near // 2
    while mask:
        gathered = jnp.concatenate([gathered, lax.ppermute(gathered, "chip", across(mask))])
        order = order + [q ^ (mask * cores) for q in order]
        mask //= 2
    gathered = jnp.concatenate([gathered, lax.ppermute(gathered, "core", other)])
    order = order + [q ^ 1 for q in order]
    slot = jnp.array([order.index(q) for q in range(n)], jnp.int32)
    order = jnp.array(order, jnp.int32)

    term_b = call(
        functools.partial(output_terms_kernel, **sizes),
        "output_terms",
        jax.ShapeDtypeStruct((n, rank, chunk), bf16),
        (strips,),
        [
            pl.BlockSpec((rank, block), lambda i, ids: (picks * block // rank, 0)),
            pl.BlockSpec((block, strip), lambda i, ids: (0, i)),
        ],
        pl.BlockSpec((per, rank, chunk), lambda i, ids: (i, 0, 0)),
        (ids,),
        (held, cotangent),
    )
    parts_b = lax.all_to_all(term_b, hid, split_axis=0, concat_axis=0, tiled=True)

    each = 4
    out_chunks = call(
        functools.partial(
            output_kernel, block=block, picks=picks, rank=rank, per=each, runs=runs, n=n
        ),
        "output_columns",
        jax.ShapeDtypeStruct((n, block, chunk), bf16),
        (n // each,),
        [whole(gathered), whole(dm), whole(do), whole(adapter_output_maps)],
        pl.BlockSpec((each, block, chunk), lambda i, *_: (i, 0, 0)),
        (ids, active, slot),
        (gathered, dm, do, adapter_output_maps),
        flops=2 * n * picks * block * block * chunk,
    )
    out_cols = lax.all_to_all(out_chunks, hid, split_axis=0, concat_axis=0, tiled=True)
    if chunk % 128 == 0:
        output = pl.pallas_call(
            functools.partial(join_copies_kernel, **sizes),
            out_shape=jax.ShapeDtypeStruct((block, model), bf16),
            in_specs=[anywhere],
            out_specs=anywhere,
            scratch_shapes=[
                pltpu.VMEM((n, block, chunk), bf16),
                pltpu.SemaphoreType.DMA((n,)),
                pltpu.SemaphoreType.DMA((n,)),
            ],
            compiler_params=pltpu.CompilerParams(vmem_limit_bytes=vmem_full),
            name="join_columns",
        )(out_cols)
    else:
        output = call(
            functools.partial(join_columns_kernel, **sizes),
            "join_columns",
            jax.ShapeDtypeStruct((block, model), bf16),
            (strips,),
            [pl.BlockSpec((per, block, chunk), lambda i, ids: (i, 0, 0))],
            pl.BlockSpec((block, strip), lambda i, ids: (0, i)),
            (ids,),
            (out_cols,),
        )

    at_rows = lambda k: pl.BlockSpec(
        (n, rank, block), lambda i, *_: (0, picks * block // rank + 1 + k, 0)
    )
    maps_a = jax.ShapeDtypeStruct(adapter_input_maps.shape, f32)
    maps_b = jax.ShapeDtypeStruct(adapter_output_maps.shape, f32)
    lanes = jax.ShapeDtypeStruct((runs, block), f32)
    grad_a, grad_b, squares = call(
        functools.partial(gradients_kernel, picks=picks, runs=runs, n=n),
        "gradients",
        (maps_a, maps_b, lanes),
        (1,),
        [at_rows(k) for k in range(picks)] + [whole(parts_b)],
        [whole(maps_a), whole(maps_b), whole(lanes)],
        (ids, active, counts, order),
        (gathered,) * picks + (parts_b,),
    )
    totals = jnp.sum(lax.all_gather(squares, hid, axis=0), axis=0)
    limit = math.sqrt(rank * (n * block + model))
    updated = call(
        functools.partial(adamw_kernel, limit=limit, runs=runs),
        "adamw",
        (maps_a,) * 3 + (maps_b,) * 3,
        (1,),
        [whole(lanes)] + [whole(maps_a)] * 4 + [whole(maps_b)] * 4,
        [whole(maps_a)] * 3 + [whole(maps_b)] * 3,
        (ids,),
        (
            totals,
            adapter_input_maps,
            first_moment_input,
            second_moment_input,
            grad_a,
            adapter_output_maps,
            first_moment_output,
            second_moment_output,
            grad_b,
        ),
    )
    return (output, *updated)


def solution(mesh):
    groups, n = mesh.devices.shape
    fine = Mesh(mesh.devices.reshape(groups, n // 2, 2), ("groups", "chip", "core"))
    hid = ("chip", "core")
    rows = P(("groups",) + hid, None)
    maps = P("groups", None, hid)
    return jax.shard_map(
        body,
        mesh=fine,
        in_specs=(rows, rows, P(None, hid), P(None, hid), P(hid, None))
        + (maps,) * 6
        + (P("groups", None), P("groups"), P(), P("groups")),
        out_specs=(rows,) + (maps,) * 6,
        check_vma=False,
    )
```

```python
import functools
import math

import jax
import jax.numpy as jnp
from jax import lax
from jax.experimental import pallas as pl
from jax.experimental.pallas import tpu as pltpu
from jax.sharding import Mesh, PartitionSpec as P

adapter_scale = 2.0 / 0.9
bf16 = jnp.bfloat16
f32 = jnp.float32
vmem_limit = 48 * 1024 * 1024
vmem_full = 62 * 1024 * 1024
strips = 8
paired_step = 4


def dot(a, b, dims=((1,), (0,))):
    return lax.dot_general(a, b, (dims, ((), ())), preferred_element_type=f32)


def call(kernel, name, out, grid, in_specs, out_specs, scalars, arrays, flops=0, moved=None):
    outs = out if isinstance(out, (tuple, list)) else [out]
    if moved is None:
        moved = sum(a.size * a.dtype.itemsize for a in (*arrays, *outs))
    return pl.pallas_call(
        kernel,
        out_shape=out,
        grid_spec=pltpu.PrefetchScalarGridSpec(
            num_scalar_prefetch=len(scalars),
            grid=grid,
            in_specs=in_specs,
            out_specs=out_specs,
        ),
        compiler_params=pltpu.CompilerParams(vmem_limit_bytes=vmem_limit),
        cost_estimate=pl.CostEstimate(flops=flops, bytes_accessed=moved, transcendentals=0),
        name=name,
    )(*scalars, *arrays)


def whole(a):
    zeros = (0,) * len(a.shape)
    return pl.BlockSpec(a.shape, lambda i, *_: zeros)


def weight_rows_kernel(gate_ref, up_ref, a_ref, o_ref, held, loads, stores, *, chunk, n, runs):
    group = lax.axis_index("groups")

    def copies(w_ref):
        return [
            pltpu.make_async_copy(
                w_ref.at[pl.ds(s * chunk, chunk)], held.at[s, pl.ds(0, chunk)], loads.at[s]
            )
            for s in range(n)
        ]

    @pl.when(group == 0)
    def _():
        for copy in copies(gate_ref):
            copy.start()

    @pl.when(group != 0)
    def _():
        for copy in copies(up_ref):
            copy.start()

    for s in range(n):
        held[s, chunk:, :] = a_ref[s * runs // n].astype(bf16)
    out = [pltpu.make_async_copy(held.at[s], o_ref.at[s], stores.at[s]) for s in range(n)]
    for s, copy in enumerate(copies(gate_ref)):
        copy.wait()
        out[s].start()
    for copy in out:
        copy.wait()


def token_columns_kernel(ids, x_ref, b_ref, o_ref, *, block, chunk, n, runs):
    per = n // strips
    for s in range(per):
        o_ref[s, :block, :] = x_ref[:, s * chunk : (s + 1) * chunk]
        run = (pl.program_id(0) * per + s) * runs // n
        o_ref[s, block:, :] = b_ref[run].astype(bf16)


def down_columns_kernel(ids, d_ref, o_ref, *, chunk, n):
    half = chunk // 2
    for s in range(n // strips):
        base = s * chunk

        @pl.when(ids[0] == 0)
        def _():
            o_ref[s] = d_ref[:, base : base + half]

        @pl.when(ids[0] != 0)
        def _():
            o_ref[s] = d_ref[:, base + half : base + chunk]


def partial_kernel(ids, active, x_ref, wm_ref, wo_ref, o_ref, *, block, chunk, picks, away):
    side = jnp.bitwise_xor(ids[1], away)
    for s in range(paired_step):
        x = x_ref[s, 0, :block, :]
        for k in range(picks):
            j = active[2 * (paired_step * pl.program_id(0) + s) + side, k]
            w = jnp.concatenate([wm_ref[j, :chunk, :], wo_ref[j, :chunk, :]], axis=1)
            o_ref[s, k] = dot(x, w).astype(o_ref.dtype)


def partial_products(ids, active, xb, wm, wo, block, chunk, away):
    n, picks = active.shape
    shape = (n // 2, picks, block, 2 * block)
    kind = bf16
    token = lambda i, ids, act: (i, jnp.bitwise_xor(ids[1], away), 0, 0)
    xp = xb.reshape(n // 2, 2, *xb.shape[1:])
    return call(
        functools.partial(partial_kernel, block=block, chunk=chunk, picks=picks, away=away),
        "gate_up_partial",
        jax.ShapeDtypeStruct(shape, kind),
        (n // 2 // paired_step,),
        [pl.BlockSpec((paired_step, 1) + xb.shape[1:], token), whole(wm), whole(wo)],
        pl.BlockSpec((paired_step,) + shape[1:], lambda i, *_: (i, 0, 0, 0)),
        (ids, active),
        (xp, wm, wo),
        moved=4096,
    )


def side_rows_kernel(ids, active, counts, seeds, *refs, block, chunk, picks, rank, n):
    b_ref, dy_ref = refs[:2]
    tile_refs, a_refs, o_ref = refs[2 : 2 + picks], refs[2 + picks : -1], refs[-1]
    total = None
    for e in range(n):
        part = dot(b_ref[e], dy_ref[:, e * chunk : (e + 1) * chunk], ((1,), (1,)))
        total = part if total is None else total + part
    for k in range(picks):
        o_ref[k * block : (k + 1) * block, :] = tile_refs[k][0].astype(f32).astype(bf16)
        base = picks * block + rank * (1 + k)
        o_ref[base : base + rank, :] = a_refs[k][0]
    base = picks * block
    o_ref[base : base + rank, :] = (adapter_scale * total).astype(bf16)


def hidden_kernel(ids, counts, r_ref, side_ref, o_ref, *, block, picks, rank):
    total = jnp.sum(r_ref[...].astype(f32), axis=0)
    swap = ids[0] != 0
    count = counts[ids[2]]
    low_t = jnp.zeros((rank, block), f32)
    own = slice(picks * block, picks * block + rank)
    for k in range(picks):
        first, second = total[k, :, :block], total[k, :, block:]
        gate = jnp.where(swap, second, first)
        up = jnp.where(swap, first, second)
        hidden = (gate / (1.0 + jnp.exp(-gate)) * up).astype(bf16)
        hidden = jnp.where(k < count, hidden, jnp.zeros_like(hidden))
        rows = slice(k * block, (k + 1) * block)
        pair = slice(picks * block + rank * (1 + k), picks * block + rank * (2 + k))
        dropped = hidden * side_ref[rows, :]
        low_t += dot(side_ref[pair, :], dropped, ((1,), (1,))).astype(bf16).astype(f32)
        o_ref[rows, :] = hidden
        o_ref[pair, :] = dot(side_ref[own, :], dropped).astype(bf16)
    o_ref[own, :] = low_t.astype(bf16)


def output_terms_kernel(ids, z_ref, dy_ref, o_ref, *, chunk, n):
    for s in range(n // strips):
        part = dot(z_ref[...], dy_ref[:, s * chunk : (s + 1) * chunk])
        o_ref[s] = (adapter_scale * part).astype(bf16)


def output_kernel(ids, active, *refs, orders, block, picks, rank, runs, n):
    h_refs, (dm_ref, do_ref, b_ref, o_ref, held, stores) = refs[: len(orders)], refs[len(orders) :]
    half = dm_ref.shape[2]
    swap = ids[0] != 0
    copies = []
    for h_ref, order in zip(h_refs, orders):
        for s, q in enumerate(order):
            t = jnp.bitwise_xor(ids[2], q)
            hidden = [h_ref[s, k * block : (k + 1) * block, :] for k in range(picks)]
            hidden = jnp.concatenate(hidden, axis=1)
            sums = []
            for d_ref in (dm_ref, do_ref):
                down = jnp.concatenate([d_ref[active[t, k]] for k in range(picks)], axis=0)
                sums.append(dot(hidden, down).astype(bf16).astype(f32))
            left = jnp.where(swap, sums[1], sums[0])
            right = jnp.where(swap, sums[0], sums[1])
            z_t = h_ref[s, picks * block : picks * block + rank, :]
            extra = adapter_scale * dot(z_t, b_ref[t * runs // n].astype(bf16), ((0,), (0,)))
            held[q, :, :half] = (left + extra[:, :half]).astype(bf16)
            held[q, :, half:] = (right + extra[:, half:]).astype(bf16)
            copy = pltpu.make_async_copy(held.at[q], o_ref.at[t], stores.at[q])
            copy.start()
            copies.append(copy)
    for copy in copies:
        copy.wait()


def join_columns_kernel(ids, c_ref, o_ref, *, chunk, n):
    for s in range(n // strips):
        o_ref[:, s * chunk : (s + 1) * chunk] = c_ref[s]


def join_copies_kernel(c_ref, o_ref, held, loads, stores, *, chunk, n):
    into = [pltpu.make_async_copy(c_ref.at[s], held.at[s], loads.at[s]) for s in range(n)]
    out = [
        pltpu.make_async_copy(held.at[s], o_ref.at[:, pl.ds(s * chunk, chunk)], stores.at[s])
        for s in range(n)
    ]
    for copy in into:
        copy.start()
    for first, second in zip(into, out):
        first.wait()
        second.start()
    for copy in out:
        copy.wait()


def gradients_kernel(ids, active, counts, *refs, orders, picks, runs, n):
    term_refs, (part_ref, ga_ref, gb_ref, sq_ref) = refs[:-4], refs[-4:]
    me = ids[2]
    per_run = n // runs
    ga_ref[...] = jnp.zeros_like(ga_ref)
    for i, order in enumerate(orders):
        for s, q in enumerate(order):
            t = jnp.bitwise_xor(me, q)
            for k in range(picks):

                @pl.when((active[t, k] == me) & (k < counts[t]))
                def _():
                    run = t * runs // n
                    ga_ref[run] = ga_ref[run] + term_refs[i * picks + k][s].astype(f32)

    for r in range(runs):
        total = part_ref[r * per_run].astype(f32)
        for q in range(1, per_run):
            total = total + part_ref[r * per_run + q].astype(f32)
        gb_ref[r] = total
        square = jnp.sum(ga_ref[r] * ga_ref[r]) + jnp.sum(total * total)
        sq_ref[r : r + 1, :] = jnp.full((1, sq_ref.shape[1]), square, f32)


def adamw_kernel(ids, sq_ref, *refs, limit, runs):
    ins, outs = refs[:8], refs[8:]
    for r in range(runs):
        factor = jnp.minimum(1.0, limit / jnp.sqrt(sq_ref[r : r + 1, :1]))
        for side in range(2):
            p_ref, m_ref, v_ref, g_ref = ins[4 * side : 4 * side + 4]
            grad = g_ref[r] * factor
            param = p_ref[r]
            moment = 0.9 * m_ref[r] + 0.1 * grad
            second = 0.999 * v_ref[r] + 0.001 * grad * grad
            corrected = moment / (1.0 - 0.9**10)
            spread = jnp.sqrt(second / (1.0 - 0.999**10)) + 1e-08
            outs[3 * side][r] = param - 0.01 * (corrected / spread + 0.1 * param)
            outs[3 * side + 1][r] = moment
            outs[3 * side + 2][r] = second


def body(
    tokens,
    cotangent,
    gate_weight,
    up_weight,
    down_weight,
    adapter_input_maps,
    adapter_output_maps,
    first_moment_input,
    second_moment_input,
    first_moment_output,
    second_moment_output,
    active,
    counts,
    dropout_tiles,
    seeds,
):
    hid = ("chip", "core")
    chips, cores = lax.axis_size("chip"), lax.axis_size("core")
    n = chips * cores
    core = lax.axis_index("core")
    me = lax.axis_index("chip") * cores + core
    ids = jnp.stack([lax.axis_index("groups"), core, me]).astype(jnp.int32)
    model = tokens.shape[1]
    tiles_n, block = dropout_tiles.shape[0], dropout_tiles.shape[1]
    picks = active.shape[1]
    runs, rank = adapter_output_maps.shape[0], adapter_output_maps.shape[1]
    chunk = model // n
    half = chunk // 2
    per = n // strips
    strip = model // strips
    other = [(0, 1), (1, 0)]
    across = lambda m: [(i, i ^ m) for i in range(chips)]
    sizes = dict(chunk=chunk, n=n)

    anywhere = pl.BlockSpec(memory_space=pl.ANY)
    w_send = pl.pallas_call(
        functools.partial(weight_rows_kernel, runs=runs, **sizes),
        out_shape=jax.ShapeDtypeStruct((n, chunk + rank, block), bf16),
        in_specs=[anywhere, anywhere, pl.BlockSpec(memory_space=pltpu.VMEM)],
        out_specs=anywhere,
        scratch_shapes=[
            pltpu.VMEM((n, chunk + rank, block), bf16),
            pltpu.SemaphoreType.DMA((n,)),
            pltpu.SemaphoreType.DMA((n,)),
        ],
        compiler_params=pltpu.CompilerParams(vmem_limit_bytes=vmem_full),
        name="weight_rows",
    )(gate_weight, up_weight, adapter_input_maps)
    wm = lax.all_to_all(w_send, hid, split_axis=0, concat_axis=0, tiled=True)
    wo = lax.ppermute(wm, "groups", other)

    x_send = call(
        functools.partial(token_columns_kernel, block=block, runs=runs, **sizes),
        "token_columns",
        jax.ShapeDtypeStruct((n, block + rank, chunk), bf16),
        (strips,),
        [pl.BlockSpec((block, strip), lambda i, ids: (0, i)), whole(adapter_output_maps)],
        pl.BlockSpec((per, block + rank, chunk), lambda i, ids: (i, 0, 0)),
        (ids,),
        (tokens, adapter_output_maps),
    )
    xb = lax.all_to_all(x_send, hid, split_axis=0, concat_axis=0, tiled=True)

    d_send = call(
        functools.partial(down_columns_kernel, **sizes),
        "down_columns",
        jax.ShapeDtypeStruct((n, block, half), bf16),
        (strips,),
        [pl.BlockSpec((block, strip), lambda i, ids: (0, i))],
        pl.BlockSpec((per, block, half), lambda i, ids: (i, 0, 0)),
        (ids,),
        (down_weight,),
    )
    d_send, xb = lax.optimization_barrier((d_send, xb))
    dm = lax.all_to_all(d_send, hid, split_axis=0, concat_axis=0, tiled=True)

    sent = partial_products(ids, active, xb, wm, wo, block, chunk, 1)
    got = lax.ppermute(sent, "core", other)
    kept = partial_products(ids, active, xb, wm, wo, block, chunk, 0)
    paired = (kept.astype(f32) + got.astype(f32)).astype(bf16)
    paired, dm = lax.optimization_barrier((paired, dm))
    far = chips // 2
    summed = lax.all_to_all(paired, "chip", split_axis=0, concat_axis=0, tiled=True)

    do = lax.ppermute(dm, "groups", other)

    rows = picks * block + rank * (1 + picks)

    def tile_spec(k):
        def at(i, ids, active, counts, seeds):
            me = ids[2]
            pick = seeds[me * runs // n] + me + 3 * active[me, k]
            return (lax.rem(pick, tiles_n), 0, 0)

        return pl.BlockSpec((1, block, block), at)

    def map_spec(k):
        return pl.BlockSpec(
            (1, rank, block), lambda i, ids, active, *_: (active[ids[2], k], chunk // rank, 0)
        )

    side = call(
        functools.partial(side_rows_kernel, block=block, picks=picks, rank=rank, **sizes),
        "side_rows",
        jax.ShapeDtypeStruct((rows, block), bf16),
        (1,),
        [
            pl.BlockSpec((n, rank, chunk), lambda i, *_: (0, block // rank, 0)),
            whole(cotangent),
        ]
        + [tile_spec(k) for k in range(picks)]
        + [map_spec(k) for k in range(picks)],
        pl.BlockSpec((rows, block), lambda i, *_: (0, 0)),
        (ids, active, counts, seeds),
        (xb, cotangent) + (dropout_tiles,) * picks + (wm,) * picks,
    )
    summed, do = lax.optimization_barrier((summed, do))
    held = call(
        functools.partial(hidden_kernel, block=block, picks=picks, rank=rank),
        "hidden_values",
        jax.ShapeDtypeStruct((rows, block), bf16),
        (1,),
        [whole(summed), whole(side)],
        pl.BlockSpec((rows, block), lambda i, *_: (0, 0)),
        (ids, counts),
        (summed, side),
    )

    term_b = call(
        functools.partial(output_terms_kernel, **sizes),
        "output_terms",
        jax.ShapeDtypeStruct((n, rank, chunk), bf16),
        (strips,),
        [
            pl.BlockSpec((rank, block), lambda i, ids: (picks * block // rank, 0)),
            pl.BlockSpec((block, strip), lambda i, ids: (0, i)),
        ],
        pl.BlockSpec((per, rank, chunk), lambda i, ids: (i, 0, 0)),
        (ids,),
        (held, cotangent),
    )

    near = chips // 4
    stack = jnp.stack(
        [held] + [lax.ppermute(held, "chip", across(m)) for m in (far, near, far + near)]
    )
    stack, term_b = lax.optimization_barrier((stack, term_b))
    parts_b = lax.all_to_all(term_b, hid, split_axis=0, concat_axis=0, tiled=True)
    pieces = [(stack, [0, far * cores, near * cores, (far + near) * cores])]
    mask = near // 2
    while mask:
        arrived = [
            (lax.ppermute(piece, "chip", across(mask)), [q ^ (mask * cores) for q in order])
            for piece, order in pieces
        ]
        pieces = pieces + arrived
        mask //= 2
    pieces = pieces + [
        (lax.ppermute(piece, "core", other), [q ^ 1 for q in order]) for piece, order in pieces
    ]
    gathered = [piece for piece, _ in pieces]
    orders = [order for _, order in pieces]

    at_once = lambda a: pl.BlockSpec(a.shape, lambda *_: (0,) * len(a.shape))
    out_chunks = pl.pallas_call(
        functools.partial(
            output_kernel, orders=orders, block=block, picks=picks, rank=rank, runs=runs, n=n
        ),
        out_shape=jax.ShapeDtypeStruct((n, block, chunk), bf16),
        grid_spec=pltpu.PrefetchScalarGridSpec(
            num_scalar_prefetch=2,
            grid=(1,),
            in_specs=[at_once(a) for a in (*gathered, dm, do, adapter_output_maps)],
            out_specs=anywhere,
            scratch_shapes=[
                pltpu.VMEM((n, block, chunk), bf16),
                pltpu.SemaphoreType.DMA((n,)),
            ],
        ),
        compiler_params=pltpu.CompilerParams(vmem_limit_bytes=vmem_limit),
        name="output_columns",
    )(ids, active, *gathered, dm, do, adapter_output_maps)
    out_cols = lax.all_to_all(out_chunks, hid, split_axis=0, concat_axis=0, tiled=True)
    if chunk % 128 == 0:
        output = pl.pallas_call(
            functools.partial(join_copies_kernel, **sizes),
            out_shape=jax.ShapeDtypeStruct((block, model), bf16),
            in_specs=[anywhere],
            out_specs=anywhere,
            scratch_shapes=[
                pltpu.VMEM((n, block, chunk), bf16),
                pltpu.SemaphoreType.DMA((n,)),
                pltpu.SemaphoreType.DMA((n,)),
            ],
            compiler_params=pltpu.CompilerParams(vmem_limit_bytes=vmem_full),
            name="join_columns",
        )(out_cols)
    else:
        output = call(
            functools.partial(join_columns_kernel, **sizes),
            "join_columns",
            jax.ShapeDtypeStruct((block, model), bf16),
            (strips,),
            [pl.BlockSpec((per, block, chunk), lambda i, ids: (i, 0, 0))],
            pl.BlockSpec((block, strip), lambda i, ids: (0, i)),
            (ids,),
            (out_cols,),
        )

    at_rows = lambda a, k: pl.BlockSpec(
        (a.shape[0], rank, block), lambda i, *_: (0, picks * block // rank + 1 + k, 0)
    )
    maps_a = jax.ShapeDtypeStruct(adapter_input_maps.shape, f32)
    maps_b = jax.ShapeDtypeStruct(adapter_output_maps.shape, f32)
    lanes = jax.ShapeDtypeStruct((runs, block), f32)
    grad_a, grad_b, squares = call(
        functools.partial(gradients_kernel, orders=orders, picks=picks, runs=runs, n=n),
        "gradients",
        (maps_a, maps_b, lanes),
        (1,),
        [at_rows(a, k) for a in gathered for k in range(picks)] + [whole(parts_b)],
        [whole(maps_a), whole(maps_b), whole(lanes)],
        (ids, active, counts),
        tuple(a for a in gathered for _ in range(picks)) + (parts_b,),
    )
    totals = jnp.sum(lax.all_gather(squares, hid, axis=0), axis=0)
    limit = math.sqrt(rank * (n * block + model))
    updated = call(
        functools.partial(adamw_kernel, limit=limit, runs=runs),
        "adamw",
        (maps_a,) * 3 + (maps_b,) * 3,
        (1,),
        [whole(lanes)] + [whole(maps_a)] * 4 + [whole(maps_b)] * 4,
        [whole(maps_a)] * 3 + [whole(maps_b)] * 3,
        (ids,),
        (
            totals,
            adapter_input_maps,
            first_moment_input,
            second_moment_input,
            grad_a,
            adapter_output_maps,
            first_moment_output,
            second_moment_output,
            grad_b,
        ),
    )
    return (output, *updated)


def solution(mesh):
    groups, n = mesh.devices.shape
    fine = Mesh(mesh.devices.reshape(groups, n // 2, 2), ("groups", "chip", "core"))
    hid = ("chip", "core")
    rows = P(("groups",) + hid, None)
    maps = P("groups", None, hid)
    return jax.shard_map(
        body,
        mesh=fine,
        in_specs=(rows, rows, P(None, hid), P(None, hid), P(hid, None))
        + (maps,) * 6
        + (P("groups", None), P("groups"), P(), P("groups")),
        out_specs=(rows,) + (maps,) * 6,
        check_vma=False,
    )
```

```python
import functools
import math

import jax
import jax.numpy as jnp
from jax import lax
from jax.experimental import pallas as pl
from jax.experimental.pallas import tpu as pltpu
from jax.sharding import Mesh, PartitionSpec as P

adapter_scale = 2.0 / 0.9
bf16 = jnp.bfloat16
f32 = jnp.float32
vmem_limit = 48 * 1024 * 1024
vmem_full = 62 * 1024 * 1024
strips = 8
paired_step = 4


def dot(a, b, dims=((1,), (0,))):
    return lax.dot_general(a, b, (dims, ((), ())), preferred_element_type=f32)


def call(kernel, name, out, grid, in_specs, out_specs, scalars, arrays, flops=0, moved=None):
    outs = out if isinstance(out, (tuple, list)) else [out]
    if moved is None:
        moved = sum(a.size * a.dtype.itemsize for a in (*arrays, *outs))
    return pl.pallas_call(
        kernel,
        out_shape=out,
        grid_spec=pltpu.PrefetchScalarGridSpec(
            num_scalar_prefetch=len(scalars),
            grid=grid,
            in_specs=in_specs,
            out_specs=out_specs,
        ),
        compiler_params=pltpu.CompilerParams(vmem_limit_bytes=vmem_limit),
        cost_estimate=pl.CostEstimate(flops=flops, bytes_accessed=moved, transcendentals=0),
        name=name,
    )(*scalars, *arrays)


def whole(a):
    zeros = (0,) * len(a.shape)
    return pl.BlockSpec(a.shape, lambda i, *_: zeros)


def weight_rows_kernel(gate_ref, up_ref, a_ref, o_ref, held, loads, stores, *, chunk, n, runs):
    group = lax.axis_index("groups")

    def copies(w_ref):
        return [
            pltpu.make_async_copy(
                w_ref.at[pl.ds(s * chunk, chunk)], held.at[s, pl.ds(0, chunk)], loads.at[s]
            )
            for s in range(n)
        ]

    @pl.when(group == 0)
    def _():
        for copy in copies(gate_ref):
            copy.start()

    @pl.when(group != 0)
    def _():
        for copy in copies(up_ref):
            copy.start()

    for s in range(n):
        held[s, chunk:, :] = a_ref[s * runs // n].astype(bf16)
    out = [pltpu.make_async_copy(held.at[s], o_ref.at[s], stores.at[s]) for s in range(n)]
    for s, copy in enumerate(copies(gate_ref)):
        copy.wait()
        out[s].start()
    for copy in out:
        copy.wait()


def token_columns_kernel(ids, x_ref, b_ref, o_ref, *, block, chunk, n, runs):
    per = n // strips
    for s in range(per):
        o_ref[s, :block, :] = x_ref[:, s * chunk : (s + 1) * chunk]
        run = (pl.program_id(0) * per + s) * runs // n
        o_ref[s, block:, :] = b_ref[run].astype(bf16)


def down_columns_kernel(ids, d_ref, o_ref, *, chunk, n):
    half = chunk // 2
    for s in range(n // strips):
        base = s * chunk

        @pl.when(ids[0] == 0)
        def _():
            o_ref[s] = d_ref[:, base : base + half]

        @pl.when(ids[0] != 0)
        def _():
            o_ref[s] = d_ref[:, base + half : base + chunk]


def partial_kernel(ids, active, x_ref, wm_ref, wo_ref, *o_refs, block, chunk, picks, first, sides):
    chip = ids[2] // 2
    for i in range(o_refs[0].shape[0]):
        for o_ref, side in zip(o_refs, sides):
            t = 2 * jnp.bitwise_xor(chip, first + i) + jnp.bitwise_xor(ids[1], side)
            x = x_ref[t, :block, :]
            for k in range(picks):
                j = active[t, k]
                w = jnp.concatenate([wm_ref[j, :chunk, :], wo_ref[j, :chunk, :]], axis=1)
                o_ref[i, k] = dot(x, w).astype(o_ref.dtype)


def partial_products(ids, active, xb, wm, wo, block, chunk, first, count, sides):
    n, picks = active.shape
    out = jax.ShapeDtypeStruct((count, picks, block, 2 * block), bf16)
    return call(
        functools.partial(
            partial_kernel, block=block, chunk=chunk, picks=picks, first=first, sides=sides
        ),
        "gate_up_partial",
        (out,) * len(sides),
        (1,),
        [pl.BlockSpec((n, block, chunk), lambda i, *_: (0, 0, 0)), whole(wm), whole(wo)],
        [whole(out)] * len(sides),
        (ids, active),
        (xb, wm, wo),
        flops=count * len(sides) * picks * 4 * block * block * chunk,
    )


def pair_sum_kernel(kept_ref, got_ref, *refs):
    o_refs, (held, stores) = refs[:-2], refs[-2:]
    copies = []
    for i, o_ref in enumerate(o_refs):
        held[i] = (kept_ref[i].astype(f32) + got_ref[i].astype(f32)).astype(bf16)
        copies.append(pltpu.make_async_copy(held.at[i], o_ref, stores.at[i]))
        copies[i].start()
    for copy in copies:
        copy.wait()


def pair_sums(kept, got):
    count = kept.shape[0]
    vmem = pl.BlockSpec(memory_space=pltpu.VMEM)
    return pl.pallas_call(
        pair_sum_kernel,
        out_shape=(jax.ShapeDtypeStruct(kept.shape[1:], bf16),) * count,
        in_specs=[vmem, vmem],
        out_specs=(pl.BlockSpec(memory_space=pltpu.HBM),) * count,
        scratch_shapes=[pltpu.VMEM(kept.shape, bf16), pltpu.SemaphoreType.DMA((count,))],
        compiler_params=pltpu.CompilerParams(vmem_limit_bytes=vmem_limit),
        name="pair_sums",
    )(kept, got)


def side_rows_kernel(ids, active, counts, seeds, *refs, block, chunk, picks, rank, n):
    b_ref, dy_ref = refs[:2]
    tile_refs, a_refs, o_ref = refs[2 : 2 + picks], refs[2 + picks : -1], refs[-1]
    total = None
    for e in range(n):
        part = dot(b_ref[e], dy_ref[:, e * chunk : (e + 1) * chunk], ((1,), (1,)))
        total = part if total is None else total + part
    for k in range(picks):
        o_ref[k * block : (k + 1) * block, :] = tile_refs[k][0].astype(f32).astype(bf16)
        base = picks * block + rank * (1 + k)
        o_ref[base : base + rank, :] = a_refs[k][0]
    base = picks * block
    o_ref[base : base + rank, :] = (adapter_scale * total).astype(bf16)


def hidden_kernel(ids, counts, *refs, block, picks, rank):
    part_refs, side_ref, o_ref = refs[:-2], refs[-2], refs[-1]
    total = part_refs[0][...].astype(f32)
    for part_ref in part_refs[1:]:
        total = total + part_ref[...].astype(f32)
    swap = ids[0] != 0
    count = counts[ids[2]]
    low_t = jnp.zeros((rank, block), f32)
    own = slice(picks * block, picks * block + rank)
    for k in range(picks):
        first, second = total[k, :, :block], total[k, :, block:]
        gate = jnp.where(swap, second, first)
        up = jnp.where(swap, first, second)
        hidden = (gate / (1.0 + jnp.exp(-gate)) * up).astype(bf16)
        hidden = jnp.where(k < count, hidden, jnp.zeros_like(hidden))
        rows = slice(k * block, (k + 1) * block)
        pair = slice(picks * block + rank * (1 + k), picks * block + rank * (2 + k))
        dropped = hidden * side_ref[rows, :]
        low_t += dot(side_ref[pair, :], dropped, ((1,), (1,))).astype(bf16).astype(f32)
        o_ref[rows, :] = hidden
        o_ref[pair, :] = dot(side_ref[own, :], dropped).astype(bf16)
    o_ref[own, :] = low_t.astype(bf16)


def output_terms_kernel(ids, z_ref, dy_ref, o_ref, *, chunk, n):
    for s in range(n):
        part = dot(z_ref[...], dy_ref[:, s * chunk : (s + 1) * chunk])
        o_ref[s] = (adapter_scale * part).astype(bf16)


def output_kernel(ids, active, *refs, orders, block, picks, rank, runs, n):
    h_refs, (dm_ref, do_ref, b_ref, o_ref, held, stores) = refs[: len(orders)], refs[len(orders) :]
    half = dm_ref.shape[2]
    swap = ids[0] != 0
    copies = []
    for h_ref, order in zip(h_refs, orders):
        for s, q in enumerate(order):
            t = jnp.bitwise_xor(ids[2], q)
            hidden = [h_ref[s, k * block : (k + 1) * block, :] for k in range(picks)]
            hidden = jnp.concatenate(hidden, axis=1)
            sums = []
            for d_ref in (dm_ref, do_ref):
                down = jnp.concatenate([d_ref[active[t, k]] for k in range(picks)], axis=0)
                sums.append(dot(hidden, down).astype(bf16).astype(f32))
            left = jnp.where(swap, sums[1], sums[0])
            right = jnp.where(swap, sums[0], sums[1])
            z_t = h_ref[s, picks * block : picks * block + rank, :]
            extra = adapter_scale * dot(z_t, b_ref[t * runs // n].astype(bf16), ((0,), (0,)))
            held[q, :, :half] = (left + extra[:, :half]).astype(bf16)
            held[q, :, half:] = (right + extra[:, half:]).astype(bf16)
            copy = pltpu.make_async_copy(held.at[q], o_ref.at[t], stores.at[q])
            copy.start()
            copies.append(copy)
    for copy in copies:
        copy.wait()


def join_columns_kernel(ids, c_ref, o_ref, *, chunk, n):
    for s in range(n // strips):
        o_ref[:, s * chunk : (s + 1) * chunk] = c_ref[s]


def join_copies_kernel(c_ref, o_ref, held, loads, stores, *, chunk, n):
    into = [pltpu.make_async_copy(c_ref.at[s], held.at[s], loads.at[s]) for s in range(n)]
    out = [
        pltpu.make_async_copy(held.at[s], o_ref.at[:, pl.ds(s * chunk, chunk)], stores.at[s])
        for s in range(n)
    ]
    for copy in into:
        copy.start()
    for first, second in zip(into, out):
        first.wait()
        second.start()
    for copy in out:
        copy.wait()


def gradients_kernel(ids, active, counts, *refs, orders, picks, runs, n):
    term_refs, (part_ref, ga_ref, gb_ref, sq_ref) = refs[:-4], refs[-4:]
    me = ids[2]
    per_run = n // runs
    ga_ref[...] = jnp.zeros_like(ga_ref)
    for i, order in enumerate(orders):
        for s, q in enumerate(order):
            t = jnp.bitwise_xor(me, q)
            for k in range(picks):

                @pl.when((active[t, k] == me) & (k < counts[t]))
                def _():
                    run = t * runs // n
                    ga_ref[run] = ga_ref[run] + term_refs[i * picks + k][s].astype(f32)

    for r in range(runs):
        total = part_ref[r * per_run].astype(f32)
        for q in range(1, per_run):
            total = total + part_ref[r * per_run + q].astype(f32)
        gb_ref[r] = total
        square = jnp.sum(ga_ref[r] * ga_ref[r]) + jnp.sum(total * total)
        sq_ref[r : r + 1, :] = jnp.full((1, sq_ref.shape[1]), square, f32)


def adamw_kernel(ids, *refs, limit, runs):
    sq_refs, ins, outs = refs[:-14], refs[-14:-6], refs[-6:]
    totals = sq_refs[0][...]
    for sq_ref in sq_refs[1:]:
        totals = totals + sq_ref[...]
    for r in range(runs):
        factor = jnp.minimum(1.0, limit / jnp.sqrt(totals[r : r + 1, :1]))
        for side in range(2):
            p_ref, m_ref, v_ref, g_ref = ins[4 * side : 4 * side + 4]
            grad = g_ref[r] * factor
            param = p_ref[r]
            moment = 0.9 * m_ref[r] + 0.1 * grad
            second = 0.999 * v_ref[r] + 0.001 * grad * grad
            corrected = moment / (1.0 - 0.9**10)
            spread = jnp.sqrt(second / (1.0 - 0.999**10)) + 1e-08
            outs[3 * side][r] = param - 0.01 * (corrected / spread + 0.1 * param)
            outs[3 * side + 1][r] = moment
            outs[3 * side + 2][r] = second


def body(
    tokens,
    cotangent,
    gate_weight,
    up_weight,
    down_weight,
    adapter_input_maps,
    adapter_output_maps,
    first_moment_input,
    second_moment_input,
    first_moment_output,
    second_moment_output,
    active,
    counts,
    dropout_tiles,
    seeds,
):
    hid = ("chip", "core")
    chips, cores = lax.axis_size("chip"), lax.axis_size("core")
    n = chips * cores
    core = lax.axis_index("core")
    me = lax.axis_index("chip") * cores + core
    ids = jnp.stack([lax.axis_index("groups"), core, me]).astype(jnp.int32)
    model = tokens.shape[1]
    tiles_n, block = dropout_tiles.shape[0], dropout_tiles.shape[1]
    picks = active.shape[1]
    runs, rank = adapter_output_maps.shape[0], adapter_output_maps.shape[1]
    chunk = model // n
    half = chunk // 2
    per = n // strips
    strip = model // strips
    other = [(0, 1), (1, 0)]
    across = lambda m: [(i, i ^ m) for i in range(chips)]
    sizes = dict(chunk=chunk, n=n)

    anywhere = pl.BlockSpec(memory_space=pl.ANY)
    w_send = pl.pallas_call(
        functools.partial(weight_rows_kernel, runs=runs, **sizes),
        out_shape=jax.ShapeDtypeStruct((n, chunk + rank, block), bf16),
        in_specs=[anywhere, anywhere, pl.BlockSpec(memory_space=pltpu.VMEM)],
        out_specs=anywhere,
        scratch_shapes=[
            pltpu.VMEM((n, chunk + rank, block), bf16),
            pltpu.SemaphoreType.DMA((n,)),
            pltpu.SemaphoreType.DMA((n,)),
        ],
        compiler_params=pltpu.CompilerParams(vmem_limit_bytes=vmem_full),
        name="weight_rows",
    )(gate_weight, up_weight, adapter_input_maps)
    wm = lax.all_to_all(w_send, hid, split_axis=0, concat_axis=0, tiled=True)
    wo = lax.ppermute(wm, "groups", other)

    x_send = call(
        functools.partial(token_columns_kernel, block=block, runs=runs, **sizes),
        "token_columns",
        jax.ShapeDtypeStruct((n, block + rank, chunk), bf16),
        (strips,),
        [pl.BlockSpec((block, strip), lambda i, ids: (0, i)), whole(adapter_output_maps)],
        pl.BlockSpec((per, block + rank, chunk), lambda i, ids: (i, 0, 0)),
        (ids,),
        (tokens, adapter_output_maps),
    )
    xb = lax.all_to_all(x_send, hid, split_axis=0, concat_axis=0, tiled=True)

    d_send = call(
        functools.partial(down_columns_kernel, **sizes),
        "down_columns",
        jax.ShapeDtypeStruct((n, block, half), bf16),
        (strips,),
        [pl.BlockSpec((block, strip), lambda i, ids: (0, i))],
        pl.BlockSpec((per, block, half), lambda i, ids: (i, 0, 0)),
        (ids,),
        (down_weight,),
    )
    d_send, xb = lax.optimization_barrier((d_send, xb))
    dm = lax.all_to_all(d_send, hid, split_axis=0, concat_axis=0, tiled=True)

    products = functools.partial(partial_products, ids, active, xb, wm, wo, block, chunk)
    far = chips // 2
    (sent,) = products(0, chips, (1,))
    got = lax.ppermute(sent, "core", other)
    (kept,) = products(0, chips, (0,))
    paired = pair_sums(kept, got)
    summed = [paired[0]] + [
        lax.ppermute(paired[c], "chip", across(c)) for c in range(1, chips)
    ]
    dm, _ = lax.optimization_barrier((dm, summed[1]))
    do = lax.ppermute(dm, "groups", other)

    rows = picks * block + rank * (1 + picks)

    def tile_spec(k):
        def at(i, ids, active, counts, seeds):
            me = ids[2]
            pick = seeds[me * runs // n] + me + 3 * active[me, k]
            return (lax.rem(pick, tiles_n), 0, 0)

        return pl.BlockSpec((1, block, block), at)

    def map_spec(k):
        return pl.BlockSpec(
            (1, rank, block), lambda i, ids, active, *_: (active[ids[2], k], chunk // rank, 0)
        )

    side = call(
        functools.partial(side_rows_kernel, block=block, picks=picks, rank=rank, **sizes),
        "side_rows",
        jax.ShapeDtypeStruct((rows, block), bf16),
        (1,),
        [
            pl.BlockSpec((n, rank, chunk), lambda i, *_: (0, block // rank, 0)),
            whole(cotangent),
        ]
        + [tile_spec(k) for k in range(picks)]
        + [map_spec(k) for k in range(picks)],
        pl.BlockSpec((rows, block), lambda i, *_: (0, 0)),
        (ids, active, counts, seeds),
        (xb, cotangent) + (dropout_tiles,) * picks + (wm,) * picks,
    )
    held = call(
        functools.partial(hidden_kernel, block=block, picks=picks, rank=rank),
        "hidden_values",
        jax.ShapeDtypeStruct((rows, block), bf16),
        (1,),
        [whole(part) for part in summed] + [whole(side)],
        pl.BlockSpec((rows, block), lambda i, *_: (0, 0)),
        (ids, counts),
        (*summed, side),
    )

    term_b = call(
        functools.partial(output_terms_kernel, **sizes),
        "output_terms",
        jax.ShapeDtypeStruct((n, rank, chunk), bf16),
        (1,),
        [
            pl.BlockSpec((rank, block), lambda i, ids: (picks * block // rank, 0)),
            whole(cotangent),
        ],
        pl.BlockSpec((n, rank, chunk), lambda i, ids: (0, 0, 0)),
        (ids,),
        (held, cotangent),
    )

    near = chips // 4
    stack = jnp.stack(
        [held] + [lax.ppermute(held, "chip", across(m)) for m in (far, near, far + near)]
    )
    stack, term_b = lax.optimization_barrier((stack, term_b))
    parts_b = lax.all_to_all(term_b, hid, split_axis=0, concat_axis=0, tiled=True)
    pieces = [(stack, [0, far * cores, near * cores, (far + near) * cores])]
    mask = near // 2
    while mask:
        arrived = [
            (lax.ppermute(piece, "chip", across(mask)), [q ^ (mask * cores) for q in order])
            for piece, order in pieces
        ]
        pieces = pieces + arrived
        mask //= 2
    pieces = pieces + [
        (lax.ppermute(piece, "core", other), [q ^ 1 for q in order]) for piece, order in pieces
    ]
    gathered = [piece for piece, _ in pieces]
    orders = [order for _, order in pieces]

    at_once = lambda a: pl.BlockSpec(a.shape, lambda *_: (0,) * len(a.shape))
    out_chunks = pl.pallas_call(
        functools.partial(
            output_kernel, orders=orders, block=block, picks=picks, rank=rank, runs=runs, n=n
        ),
        out_shape=jax.ShapeDtypeStruct((n, block, chunk), bf16),
        grid_spec=pltpu.PrefetchScalarGridSpec(
            num_scalar_prefetch=2,
            grid=(1,),
            in_specs=[at_once(a) for a in (*gathered, dm, do, adapter_output_maps)],
            out_specs=anywhere,
            scratch_shapes=[
                pltpu.VMEM((n, block, chunk), bf16),
                pltpu.SemaphoreType.DMA((n,)),
            ],
        ),
        compiler_params=pltpu.CompilerParams(vmem_limit_bytes=vmem_limit),
        name="output_columns",
    )(ids, active, *gathered, dm, do, adapter_output_maps)
    out_cols = lax.all_to_all(out_chunks, hid, split_axis=0, concat_axis=0, tiled=True)
    if chunk % 128 == 0:
        output = pl.pallas_call(
            functools.partial(join_copies_kernel, **sizes),
            out_shape=jax.ShapeDtypeStruct((block, model), bf16),
            in_specs=[anywhere],
            out_specs=anywhere,
            scratch_shapes=[
                pltpu.VMEM((n, block, chunk), bf16),
                pltpu.SemaphoreType.DMA((n,)),
                pltpu.SemaphoreType.DMA((n,)),
            ],
            compiler_params=pltpu.CompilerParams(vmem_limit_bytes=vmem_full),
            name="join_columns",
        )(out_cols)
    else:
        output = call(
            functools.partial(join_columns_kernel, **sizes),
            "join_columns",
            jax.ShapeDtypeStruct((block, model), bf16),
            (strips,),
            [pl.BlockSpec((per, block, chunk), lambda i, ids: (i, 0, 0))],
            pl.BlockSpec((block, strip), lambda i, ids: (0, i)),
            (ids,),
            (out_cols,),
        )

    at_rows = lambda a, k: pl.BlockSpec(
        (a.shape[0], rank, block), lambda i, *_: (0, picks * block // rank + 1 + k, 0)
    )
    maps_a = jax.ShapeDtypeStruct(adapter_input_maps.shape, f32)
    maps_b = jax.ShapeDtypeStruct(adapter_output_maps.shape, f32)
    lanes = jax.ShapeDtypeStruct((runs, block), f32)
    grad_a, grad_b, squares = call(
        functools.partial(gradients_kernel, orders=orders, picks=picks, runs=runs, n=n),
        "gradients",
        (maps_a, maps_b, lanes),
        (1,),
        [at_rows(a, k) for a in gathered for k in range(picks)] + [whole(parts_b)],
        [whole(maps_a), whole(maps_b), whole(lanes)],
        (ids, active, counts),
        tuple(a for a in gathered for _ in range(picks)) + (parts_b,),
    )
    squares = squares + lax.ppermute(squares, "core", other)
    totals = [squares] + [lax.ppermute(squares, "chip", across(c)) for c in range(1, chips)]
    limit = math.sqrt(rank * (n * block + model))
    updated = call(
        functools.partial(adamw_kernel, limit=limit, runs=runs),
        "adamw",
        (maps_a,) * 3 + (maps_b,) * 3,
        (1,),
        [whole(lanes)] * chips + [whole(maps_a)] * 4 + [whole(maps_b)] * 4,
        [whole(maps_a)] * 3 + [whole(maps_b)] * 3,
        (ids,),
        (
            *totals,
            adapter_input_maps,
            first_moment_input,
            second_moment_input,
            grad_a,
            adapter_output_maps,
            first_moment_output,
            second_moment_output,
            grad_b,
        ),
    )
    return (output, *updated)


def solution(mesh):
    groups, n = mesh.devices.shape
    fine = Mesh(mesh.devices.reshape(groups, n // 2, 2), ("groups", "chip", "core"))
    hid = ("chip", "core")
    rows = P(("groups",) + hid, None)
    maps = P("groups", None, hid)
    return jax.shard_map(
        body,
        mesh=fine,
        in_specs=(rows, rows, P(None, hid), P(None, hid), P(hid, None))
        + (maps,) * 6
        + (P("groups", None), P("groups"), P(), P("groups")),
        out_specs=(rows,) + (maps,) * 6,
        check_vma=False,
    )
```

```python
import functools
import math

import jax
import jax.numpy as jnp
from jax import lax
from jax.experimental import pallas as pl
from jax.experimental.pallas import tpu as pltpu
from jax.sharding import Mesh, PartitionSpec as P

adapter_scale = 2.0 / 0.9
bf16 = jnp.bfloat16
f32 = jnp.float32
vmem_limit = 48 * 1024 * 1024
vmem_full = 62 * 1024 * 1024
strips = 8
paired_step = 4


def dot(a, b, dims=((1,), (0,))):
    return lax.dot_general(a, b, (dims, ((), ())), preferred_element_type=f32)


def call(kernel, name, out, grid, in_specs, out_specs, scalars, arrays, flops=0, moved=None):
    outs = out if isinstance(out, (tuple, list)) else [out]
    if moved is None:
        moved = sum(a.size * a.dtype.itemsize for a in (*arrays, *outs))
    return pl.pallas_call(
        kernel,
        out_shape=out,
        grid_spec=pltpu.PrefetchScalarGridSpec(
            num_scalar_prefetch=len(scalars),
            grid=grid,
            in_specs=in_specs,
            out_specs=out_specs,
        ),
        compiler_params=pltpu.CompilerParams(vmem_limit_bytes=vmem_limit),
        cost_estimate=pl.CostEstimate(flops=flops, bytes_accessed=moved, transcendentals=0),
        name=name,
    )(*scalars, *arrays)


def whole(a):
    zeros = (0,) * len(a.shape)
    return pl.BlockSpec(a.shape, lambda i, *_: zeros)


def weight_rows_kernel(gate_ref, up_ref, a_ref, o_ref, held, loads, stores, *, chunk, n, runs):
    group = lax.axis_index("groups")

    def copies(w_ref):
        return [
            pltpu.make_async_copy(
                w_ref.at[pl.ds(s * chunk, chunk)], held.at[s, pl.ds(0, chunk)], loads.at[s]
            )
            for s in range(n)
        ]

    @pl.when(group == 0)
    def _():
        for copy in copies(gate_ref):
            copy.start()

    @pl.when(group != 0)
    def _():
        for copy in copies(up_ref):
            copy.start()

    for s in range(n):
        held[s, chunk:, :] = a_ref[s * runs // n].astype(bf16)
    out = [pltpu.make_async_copy(held.at[s], o_ref.at[s], stores.at[s]) for s in range(n)]
    for s, copy in enumerate(copies(gate_ref)):
        copy.wait()
        out[s].start()
    for copy in out:
        copy.wait()


def token_columns_kernel(ids, x_ref, b_ref, o_ref, *, block, chunk, n, runs):
    per = n // strips
    for s in range(per):
        o_ref[s, :block, :] = x_ref[:, s * chunk : (s + 1) * chunk]
        run = (pl.program_id(0) * per + s) * runs // n
        o_ref[s, block:, :] = b_ref[run].astype(bf16)


def down_columns_kernel(ids, d_ref, o_ref, *, chunk, n):
    half = chunk // 2
    for s in range(n // strips):
        base = s * chunk

        @pl.when(ids[0] == 0)
        def _():
            o_ref[s] = d_ref[:, base : base + half]

        @pl.when(ids[0] != 0)
        def _():
            o_ref[s] = d_ref[:, base + half : base + chunk]


def partial_kernel(ids, active, x_ref, wm_ref, wo_ref, *o_refs, block, chunk, picks, first, sides):
    chip = ids[2] // 2
    for i in range(o_refs[0].shape[0]):
        for o_ref, side in zip(o_refs, sides):
            t = 2 * jnp.bitwise_xor(chip, first + i) + jnp.bitwise_xor(ids[1], side)
            x = x_ref[t, :block, :]
            for k in range(picks):
                j = active[t, k]
                w = jnp.concatenate([wm_ref[j, :chunk, :], wo_ref[j, :chunk, :]], axis=1)
                o_ref[i, k] = dot(x, w).astype(o_ref.dtype)


def partial_products(ids, active, xb, wm, wo, block, chunk, first, count, sides):
    n, picks = active.shape
    out = jax.ShapeDtypeStruct((count, picks, block, 2 * block), bf16)
    return call(
        functools.partial(
            partial_kernel, block=block, chunk=chunk, picks=picks, first=first, sides=sides
        ),
        "gate_up_partial",
        (out,) * len(sides),
        (1,),
        [pl.BlockSpec((n, block, chunk), lambda i, *_: (0, 0, 0)), whole(wm), whole(wo)],
        [whole(out)] * len(sides),
        (ids, active),
        (xb, wm, wo),
        flops=count * len(sides) * picks * 4 * block * block * chunk,
    )


def pair_sum_kernel(kept_ref, got_ref, *refs, places):
    o_refs, (held, stores) = refs[:-2], refs[-2:]
    copies = []
    for i, (out, at) in enumerate(places):
        held[i] = (kept_ref[i].astype(f32) + got_ref[i].astype(f32)).astype(bf16)
        copies.append(pltpu.make_async_copy(held.at[i], o_refs[out].at[at], stores.at[i]))
        copies[i].start()
    for copy in copies:
        copy.wait()


def pair_sums(kept, got, places):
    count = kept.shape[0]
    outs = 1 + max(out for out, _ in places)
    vmem = pl.BlockSpec(memory_space=pltpu.VMEM)
    return pl.pallas_call(
        functools.partial(pair_sum_kernel, places=places),
        out_shape=(jax.ShapeDtypeStruct((count // outs,) + kept.shape[1:], bf16),) * outs,
        in_specs=[vmem, vmem],
        out_specs=(pl.BlockSpec(memory_space=pltpu.HBM),) * outs,
        scratch_shapes=[pltpu.VMEM(kept.shape, bf16), pltpu.SemaphoreType.DMA((count,))],
        compiler_params=pltpu.CompilerParams(vmem_limit_bytes=vmem_limit),
        name="pair_sums",
    )(kept, got)


def side_rows_kernel(ids, active, counts, seeds, *refs, block, chunk, picks, rank, n):
    b_ref, dy_ref = refs[:2]
    tile_refs, a_refs, o_ref = refs[2 : 2 + picks], refs[2 + picks : -1], refs[-1]
    total = None
    for e in range(n):
        part = dot(b_ref[e], dy_ref[:, e * chunk : (e + 1) * chunk], ((1,), (1,)))
        total = part if total is None else total + part
    for k in range(picks):
        o_ref[k * block : (k + 1) * block, :] = tile_refs[k][0].astype(f32).astype(bf16)
        base = picks * block + rank * (1 + k)
        o_ref[base : base + rank, :] = a_refs[k][0]
    base = picks * block
    o_ref[base : base + rank, :] = (adapter_scale * total).astype(bf16)


def hidden_kernel(ids, counts, *refs, block, picks, rank):
    part_refs, side_ref, o_ref = refs[:-2], refs[-2], refs[-1]
    total = part_refs[0][0].astype(f32)
    for part_ref in part_refs[1:]:
        total = total + part_ref[0].astype(f32)
    swap = ids[0] != 0
    count = counts[ids[2]]
    low_t = jnp.zeros((rank, block), f32)
    own = slice(picks * block, picks * block + rank)
    for k in range(picks):
        first, second = total[k, :, :block], total[k, :, block:]
        gate = jnp.where(swap, second, first)
        up = jnp.where(swap, first, second)
        hidden = (gate / (1.0 + jnp.exp(-gate)) * up).astype(bf16)
        hidden = jnp.where(k < count, hidden, jnp.zeros_like(hidden))
        rows = slice(k * block, (k + 1) * block)
        pair = slice(picks * block + rank * (1 + k), picks * block + rank * (2 + k))
        dropped = hidden * side_ref[rows, :]
        low_t += dot(side_ref[pair, :], dropped, ((1,), (1,))).astype(bf16).astype(f32)
        o_ref[rows, :] = hidden
        o_ref[pair, :] = dot(side_ref[own, :], dropped).astype(bf16)
    o_ref[own, :] = low_t.astype(bf16)


def output_terms_kernel(ids, z_ref, dy_ref, o_ref, *, chunk, n):
    for s in range(n):
        part = dot(z_ref[...], dy_ref[:, s * chunk : (s + 1) * chunk])
        o_ref[s] = (adapter_scale * part).astype(bf16)


def output_kernel(ids, active, *refs, orders, block, picks, rank, runs, n):
    h_refs, (dm_ref, do_ref, b_ref, o_ref, held, stores) = refs[: len(orders)], refs[len(orders) :]
    half = dm_ref.shape[2]
    swap = ids[0] != 0
    copies = []
    for h_ref, order in zip(h_refs, orders):
        for s, q in enumerate(order):
            t = jnp.bitwise_xor(ids[2], q)
            hidden = [h_ref[s, k * block : (k + 1) * block, :] for k in range(picks)]
            hidden = jnp.concatenate(hidden, axis=1)
            sums = []
            for d_ref in (dm_ref, do_ref):
                down = jnp.concatenate([d_ref[active[t, k]] for k in range(picks)], axis=0)
                sums.append(dot(hidden, down).astype(bf16).astype(f32))
            left = jnp.where(swap, sums[1], sums[0])
            right = jnp.where(swap, sums[0], sums[1])
            z_t = h_ref[s, picks * block : picks * block + rank, :]
            extra = adapter_scale * dot(z_t, b_ref[t * runs // n].astype(bf16), ((0,), (0,)))
            held[q, :, :half] = (left + extra[:, :half]).astype(bf16)
            held[q, :, half:] = (right + extra[:, half:]).astype(bf16)
            copy = pltpu.make_async_copy(held.at[q], o_ref.at[t], stores.at[q])
            copy.start()
            copies.append(copy)
    for copy in copies:
        copy.wait()


def join_columns_kernel(ids, c_ref, o_ref, *, chunk, n):
    for s in range(n // strips):
        o_ref[:, s * chunk : (s + 1) * chunk] = c_ref[s]


def join_copies_kernel(c_ref, o_ref, held, loads, stores, *, chunk, n):
    into = [pltpu.make_async_copy(c_ref.at[s], held.at[s], loads.at[s]) for s in range(n)]
    out = [
        pltpu.make_async_copy(held.at[s], o_ref.at[:, pl.ds(s * chunk, chunk)], stores.at[s])
        for s in range(n)
    ]
    for copy in into:
        copy.start()
    for first, second in zip(into, out):
        first.wait()
        second.start()
    for copy in out:
        copy.wait()


def gradients_kernel(ids, active, counts, *refs, orders, picks, runs, n):
    term_refs, (part_ref, ga_ref, gb_ref, sq_ref) = refs[:-4], refs[-4:]
    me = ids[2]
    per_run = n // runs
    ga_ref[...] = jnp.zeros_like(ga_ref)
    for i, order in enumerate(orders):
        for s, q in enumerate(order):
            t = jnp.bitwise_xor(me, q)
            for k in range(picks):

                @pl.when((active[t, k] == me) & (k < counts[t]))
                def _():
                    run = t * runs // n
                    ga_ref[run] = ga_ref[run] + term_refs[i * picks + k][s].astype(f32)

    for r in range(runs):
        total = part_ref[r * per_run].astype(f32)
        for q in range(1, per_run):
            total = total + part_ref[r * per_run + q].astype(f32)
        gb_ref[r] = total
        square = jnp.sum(ga_ref[r] * ga_ref[r]) + jnp.sum(total * total)
        sq_ref[r : r + 1, :] = jnp.full((1, sq_ref.shape[1]), square, f32)


def adamw_kernel(ids, *refs, limit, runs):
    sq_refs, ins, outs = refs[:-14], refs[-14:-6], refs[-6:]
    totals = sq_refs[0][...]
    for sq_ref in sq_refs[1:]:
        totals = totals + sq_ref[...]
    for r in range(runs):
        factor = jnp.minimum(1.0, limit / jnp.sqrt(totals[r : r + 1, :1]))
        for side in range(2):
            p_ref, m_ref, v_ref, g_ref = ins[4 * side : 4 * side + 4]
            grad = g_ref[r] * factor
            param = p_ref[r]
            moment = 0.9 * m_ref[r] + 0.1 * grad
            second = 0.999 * v_ref[r] + 0.001 * grad * grad
            corrected = moment / (1.0 - 0.9**10)
            spread = jnp.sqrt(second / (1.0 - 0.999**10)) + 1e-08
            outs[3 * side][r] = param - 0.01 * (corrected / spread + 0.1 * param)
            outs[3 * side + 1][r] = moment
            outs[3 * side + 2][r] = second


def body(
    tokens,
    cotangent,
    gate_weight,
    up_weight,
    down_weight,
    adapter_input_maps,
    adapter_output_maps,
    first_moment_input,
    second_moment_input,
    first_moment_output,
    second_moment_output,
    active,
    counts,
    dropout_tiles,
    seeds,
):
    hid = ("chip", "core")
    chips, cores = lax.axis_size("chip"), lax.axis_size("core")
    n = chips * cores
    core = lax.axis_index("core")
    me = lax.axis_index("chip") * cores + core
    ids = jnp.stack([lax.axis_index("groups"), core, me]).astype(jnp.int32)
    model = tokens.shape[1]
    tiles_n, block = dropout_tiles.shape[0], dropout_tiles.shape[1]
    picks = active.shape[1]
    runs, rank = adapter_output_maps.shape[0], adapter_output_maps.shape[1]
    chunk = model // n
    half = chunk // 2
    per = n // strips
    strip = model // strips
    other = [(0, 1), (1, 0)]
    across = lambda m: [(i, i ^ m) for i in range(chips)]
    sizes = dict(chunk=chunk, n=n)

    anywhere = pl.BlockSpec(memory_space=pl.ANY)
    w_send = pl.pallas_call(
        functools.partial(weight_rows_kernel, runs=runs, **sizes),
        out_shape=jax.ShapeDtypeStruct((n, chunk + rank, block), bf16),
        in_specs=[anywhere, anywhere, pl.BlockSpec(memory_space=pltpu.VMEM)],
        out_specs=anywhere,
        scratch_shapes=[
            pltpu.VMEM((n, chunk + rank, block), bf16),
            pltpu.SemaphoreType.DMA((n,)),
            pltpu.SemaphoreType.DMA((n,)),
        ],
        compiler_params=pltpu.CompilerParams(vmem_limit_bytes=vmem_full),
        name="weight_rows",
    )(gate_weight, up_weight, adapter_input_maps)
    wm = lax.all_to_all(w_send, hid, split_axis=0, concat_axis=0, tiled=True)
    wo = lax.ppermute(wm, "groups", other)

    x_send = call(
        functools.partial(token_columns_kernel, block=block, runs=runs, **sizes),
        "token_columns",
        jax.ShapeDtypeStruct((n, block + rank, chunk), bf16),
        (strips,),
        [pl.BlockSpec((block, strip), lambda i, ids: (0, i)), whole(adapter_output_maps)],
        pl.BlockSpec((per, block + rank, chunk), lambda i, ids: (i, 0, 0)),
        (ids,),
        (tokens, adapter_output_maps),
    )
    xb = lax.all_to_all(x_send, hid, split_axis=0, concat_axis=0, tiled=True)

    d_send = call(
        functools.partial(down_columns_kernel, **sizes),
        "down_columns",
        jax.ShapeDtypeStruct((n, block, half), bf16),
        (strips,),
        [pl.BlockSpec((block, strip), lambda i, ids: (0, i))],
        pl.BlockSpec((per, block, half), lambda i, ids: (i, 0, 0)),
        (ids,),
        (down_weight,),
    )
    d_send, xb = lax.optimization_barrier((d_send, xb))
    dm = lax.all_to_all(d_send, hid, split_axis=0, concat_axis=0, tiled=True)

    products = functools.partial(partial_products, ids, active, xb, wm, wo, block, chunk)
    far = chips // 2
    (sent,) = products(0, chips, (1,))
    got = lax.ppermute(sent, "core", other)
    (kept,) = products(0, chips, (0,))
    x_kept, x_sent = pair_sums(kept, got, [(c % 2, c // 2) for c in range(chips)])
    x_got = lax.ppermute(x_sent, "chip", across(1))
    paired = pair_sums(x_kept, x_got, [(c, 0) for c in range(chips // 2)])
    summed = [paired[0]] + [
        lax.ppermute(paired[c], "chip", across(2 * c)) for c in range(1, chips // 2)
    ]
    dm, _ = lax.optimization_barrier((dm, x_got))
    do = lax.ppermute(dm, "groups", other)

    rows = picks * block + rank * (1 + picks)

    def tile_spec(k):
        def at(i, ids, active, counts, seeds):
            me = ids[2]
            pick = seeds[me * runs // n] + me + 3 * active[me, k]
            return (lax.rem(pick, tiles_n), 0, 0)

        return pl.BlockSpec((1, block, block), at)

    def map_spec(k):
        return pl.BlockSpec(
            (1, rank, block), lambda i, ids, active, *_: (active[ids[2], k], chunk // rank, 0)
        )

    side = call(
        functools.partial(side_rows_kernel, block=block, picks=picks, rank=rank, **sizes),
        "side_rows",
        jax.ShapeDtypeStruct((rows, block), bf16),
        (1,),
        [
            pl.BlockSpec((n, rank, chunk), lambda i, *_: (0, block // rank, 0)),
            whole(cotangent),
        ]
        + [tile_spec(k) for k in range(picks)]
        + [map_spec(k) for k in range(picks)],
        pl.BlockSpec((rows, block), lambda i, *_: (0, 0)),
        (ids, active, counts, seeds),
        (xb, cotangent) + (dropout_tiles,) * picks + (wm,) * picks,
    )
    held = call(
        functools.partial(hidden_kernel, block=block, picks=picks, rank=rank),
        "hidden_values",
        jax.ShapeDtypeStruct((rows, block), bf16),
        (1,),
        [whole(part) for part in summed] + [whole(side)],
        pl.BlockSpec((rows, block), lambda i, *_: (0, 0)),
        (ids, counts),
        (*summed, side),
    )

    term_b = call(
        functools.partial(output_terms_kernel, **sizes),
        "output_terms",
        jax.ShapeDtypeStruct((n, rank, chunk), bf16),
        (1,),
        [
            pl.BlockSpec((rank, block), lambda i, ids: (picks * block // rank, 0)),
            whole(cotangent),
        ],
        pl.BlockSpec((n, rank, chunk), lambda i, ids: (0, 0, 0)),
        (ids,),
        (held, cotangent),
    )

    near = chips // 4
    stack = jnp.stack(
        [held] + [lax.ppermute(held, "chip", across(m)) for m in (far, near, far + near)]
    )
    stack, term_b = lax.optimization_barrier((stack, term_b))
    parts_b = lax.all_to_all(term_b, hid, split_axis=0, concat_axis=0, tiled=True)
    pieces = [(stack, [0, far * cores, near * cores, (far + near) * cores])]
    mask = near // 2
    while mask:
        arrived = [
            (lax.ppermute(piece, "chip", across(mask)), [q ^ (mask * cores) for q in order])
            for piece, order in pieces
        ]
        pieces = pieces + arrived
        mask //= 2
    pieces = pieces + [
        (lax.ppermute(piece, "core", other), [q ^ 1 for q in order]) for piece, order in pieces
    ]
    gathered = [piece for piece, _ in pieces]
    orders = [order for _, order in pieces]

    at_once = lambda a: pl.BlockSpec(a.shape, lambda *_: (0,) * len(a.shape))
    out_chunks = pl.pallas_call(
        functools.partial(
            output_kernel, orders=orders, block=block, picks=picks, rank=rank, runs=runs, n=n
        ),
        out_shape=jax.ShapeDtypeStruct((n, block, chunk), bf16),
        grid_spec=pltpu.PrefetchScalarGridSpec(
            num_scalar_prefetch=2,
            grid=(1,),
            in_specs=[at_once(a) for a in (*gathered, dm, do, adapter_output_maps)],
            out_specs=anywhere,
            scratch_shapes=[
                pltpu.VMEM((n, block, chunk), bf16),
                pltpu.SemaphoreType.DMA((n,)),
            ],
        ),
        compiler_params=pltpu.CompilerParams(vmem_limit_bytes=vmem_limit),
        name="output_columns",
    )(ids, active, *gathered, dm, do, adapter_output_maps)
    out_cols = lax.all_to_all(out_chunks, hid, split_axis=0, concat_axis=0, tiled=True)
    if chunk % 128 == 0:
        output = pl.pallas_call(
            functools.partial(join_copies_kernel, **sizes),
            out_shape=jax.ShapeDtypeStruct((block, model), bf16),
            in_specs=[anywhere],
            out_specs=anywhere,
            scratch_shapes=[
                pltpu.VMEM((n, block, chunk), bf16),
                pltpu.SemaphoreType.DMA((n,)),
                pltpu.SemaphoreType.DMA((n,)),
            ],
            compiler_params=pltpu.CompilerParams(vmem_limit_bytes=vmem_full),
            name="join_columns",
        )(out_cols)
    else:
        output = call(
            functools.partial(join_columns_kernel, **sizes),
            "join_columns",
            jax.ShapeDtypeStruct((block, model), bf16),
            (strips,),
            [pl.BlockSpec((per, block, chunk), lambda i, ids: (i, 0, 0))],
            pl.BlockSpec((block, strip), lambda i, ids: (0, i)),
            (ids,),
            (out_cols,),
        )

    at_rows = lambda a, k: pl.BlockSpec(
        (a.shape[0], rank, block), lambda i, *_: (0, picks * block // rank + 1 + k, 0)
    )
    maps_a = jax.ShapeDtypeStruct(adapter_input_maps.shape, f32)
    maps_b = jax.ShapeDtypeStruct(adapter_output_maps.shape, f32)
    lanes = jax.ShapeDtypeStruct((runs, block), f32)
    grad_a, grad_b, squares = call(
        functools.partial(gradients_kernel, orders=orders, picks=picks, runs=runs, n=n),
        "gradients",
        (maps_a, maps_b, lanes),
        (1,),
        [at_rows(a, k) for a in gathered for k in range(picks)] + [whole(parts_b)],
        [whole(maps_a), whole(maps_b), whole(lanes)],
        (ids, active, counts),
        tuple(a for a in gathered for _ in range(picks)) + (parts_b,),
    )
    squares = squares + lax.ppermute(squares, "core", other)
    mask = 1
    while mask < near:
        squares = squares + lax.ppermute(squares, "chip", across(mask))
        mask *= 2
    totals = [squares] + [
        lax.ppermute(squares, "chip", across(m)) for m in (far, near, far + near)
    ]
    totals, output = lax.optimization_barrier((totals, output))
    limit = math.sqrt(rank * (n * block + model))
    updated = call(
        functools.partial(adamw_kernel, limit=limit, runs=runs),
        "adamw",
        (maps_a,) * 3 + (maps_b,) * 3,
        (1,),
        [whole(lanes)] * len(totals) + [whole(maps_a)] * 4 + [whole(maps_b)] * 4,
        [whole(maps_a)] * 3 + [whole(maps_b)] * 3,
        (ids,),
        (
            *totals,
            adapter_input_maps,
            first_moment_input,
            second_moment_input,
            grad_a,
            adapter_output_maps,
            first_moment_output,
            second_moment_output,
            grad_b,
        ),
    )
    return (output, *updated)


def solution(mesh):
    groups, n = mesh.devices.shape
    fine = Mesh(mesh.devices.reshape(groups, n // 2, 2), ("groups", "chip", "core"))
    hid = ("chip", "core")
    rows = P(("groups",) + hid, None)
    maps = P("groups", None, hid)
    return jax.shard_map(
        body,
        mesh=fine,
        in_specs=(rows, rows, P(None, hid), P(None, hid), P(hid, None))
        + (maps,) * 6
        + (P("groups", None), P("groups"), P(), P("groups")),
        out_specs=(rows,) + (maps,) * 6,
        check_vma=False,
    )
```

```python
import functools
import math

import jax
import jax.numpy as jnp
from jax import lax
from jax.experimental import pallas as pl
from jax.experimental.pallas import tpu as pltpu
from jax.sharding import Mesh, PartitionSpec as P

adapter_scale = 2.0 / 0.9
bf16 = jnp.bfloat16
f32 = jnp.float32
vmem_limit = 48 * 1024 * 1024
vmem_full = 62 * 1024 * 1024
strips = 8
paired_step = 4


def dot(a, b, dims=((1,), (0,))):
    return lax.dot_general(a, b, (dims, ((), ())), preferred_element_type=f32)


def call(kernel, name, out, grid, in_specs, out_specs, scalars, arrays, flops=0, moved=None):
    outs = out if isinstance(out, (tuple, list)) else [out]
    if moved is None:
        moved = sum(a.size * a.dtype.itemsize for a in (*arrays, *outs))
    return pl.pallas_call(
        kernel,
        out_shape=out,
        grid_spec=pltpu.PrefetchScalarGridSpec(
            num_scalar_prefetch=len(scalars),
            grid=grid,
            in_specs=in_specs,
            out_specs=out_specs,
        ),
        compiler_params=pltpu.CompilerParams(vmem_limit_bytes=vmem_limit),
        cost_estimate=pl.CostEstimate(flops=flops, bytes_accessed=moved, transcendentals=0),
        name=name,
    )(*scalars, *arrays)


def whole(a):
    zeros = (0,) * len(a.shape)
    return pl.BlockSpec(a.shape, lambda i, *_: zeros)


def weight_rows_kernel(
    gate_ref, up_ref, a_ref, o_ref, held, maps, loads, stores, *, chunk, n, runs
):
    group = lax.axis_index("groups")

    def copies(w_ref):
        return [
            pltpu.make_async_copy(
                w_ref.at[pl.ds(s * chunk, chunk)], held.at[s, pl.ds(0, chunk)], loads.at[s]
            )
            for s in range(n)
        ]

    @pl.when(group == 0)
    def _():
        for copy in copies(gate_ref):
            copy.start()

    @pl.when(group != 0)
    def _():
        for copy in copies(up_ref):
            copy.start()

    fetch = pltpu.make_async_copy(a_ref, maps, loads.at[n])
    fetch.start()
    fetch.wait()
    for s in range(n):
        held[s, chunk:, :] = maps[s * runs // n].astype(bf16)
    out = [pltpu.make_async_copy(held.at[s], o_ref.at[s], stores.at[s]) for s in range(n)]
    for s, copy in enumerate(copies(gate_ref)):
        copy.wait()
        out[s].start()
    for copy in out:
        copy.wait()


def token_columns_kernel(ids, x_ref, o_ref, *, chunk, n):
    for s in range(n // strips):
        o_ref[s] = x_ref[:, s * chunk : (s + 1) * chunk]


def down_columns_kernel(ids, d_ref, b_ref, o_ref, *, block, chunk, rank, n, runs):
    half, part = chunk // 2, rank // 2
    per = n // strips
    for s in range(per):
        base = s * chunk

        @pl.when(ids[0] == 0)
        def _():
            o_ref[s, :block, :] = d_ref[:, base : base + half]

        @pl.when(ids[0] != 0)
        def _():
            o_ref[s, :block, :] = d_ref[:, base + half : base + chunk]

        run = (pl.program_id(0) * per + s) * runs // n
        mine = b_ref[run, (s % 2) * part : (s % 2 + 1) * part, :]
        o_ref[s, block:, :] = jnp.concatenate([mine[:, :half], mine[:, half:]]).astype(bf16)


def partial_kernel(ids, active, x_ref, wm_ref, wo_ref, *o_refs, block, chunk, picks, first, sides):
    chip = ids[2] // 2
    for i in range(o_refs[0].shape[0]):
        for o_ref, side in zip(o_refs, sides):
            t = 2 * jnp.bitwise_xor(chip, first + i) + jnp.bitwise_xor(ids[1], side)
            x = x_ref[t, :block, :]
            for k in range(picks):
                j = active[t, k]
                w = jnp.concatenate([wm_ref[j, :chunk, :], wo_ref[j, :chunk, :]], axis=1)
                o_ref[i, k] = dot(x, w).astype(o_ref.dtype)


def partial_products(ids, active, xb, wm, wo, block, chunk, first, count, sides):
    n, picks = active.shape
    out = jax.ShapeDtypeStruct((count, picks, block, 2 * block), bf16)
    return call(
        functools.partial(
            partial_kernel, block=block, chunk=chunk, picks=picks, first=first, sides=sides
        ),
        "gate_up_partial",
        (out,) * len(sides),
        (1,),
        [pl.BlockSpec((n, block, chunk), lambda i, *_: (0, 0, 0)), whole(wm), whole(wo)],
        [whole(out)] * len(sides),
        (ids, active),
        (xb, wm, wo),
        flops=count * len(sides) * picks * 4 * block * block * chunk,
    )


def pair_sum_kernel(kept_ref, got_ref, *refs, places):
    o_refs, (held, stores) = refs[:-2], refs[-2:]
    copies = []
    for i, (out, at) in enumerate(places):
        held[i] = (kept_ref[i].astype(f32) + got_ref[i].astype(f32)).astype(bf16)
        copies.append(pltpu.make_async_copy(held.at[i], o_refs[out].at[at], stores.at[i]))
        copies[i].start()
    for copy in copies:
        copy.wait()


def pair_sums(kept, got, places):
    count = kept.shape[0]
    outs = 1 + max(out for out, _ in places)
    vmem = pl.BlockSpec(memory_space=pltpu.VMEM)
    return pl.pallas_call(
        functools.partial(pair_sum_kernel, places=places),
        out_shape=(jax.ShapeDtypeStruct((count // outs,) + kept.shape[1:], bf16),) * outs,
        in_specs=[vmem, vmem],
        out_specs=(pl.BlockSpec(memory_space=pltpu.HBM),) * outs,
        scratch_shapes=[pltpu.VMEM(kept.shape, bf16), pltpu.SemaphoreType.DMA((count,))],
        compiler_params=pltpu.CompilerParams(vmem_limit_bytes=vmem_limit),
        name="pair_sums",
    )(kept, got)


def side_rows_kernel(ids, active, counts, seeds, *refs, block, chunk, picks, rank, n):
    own_ref, got_ref, dy_ref = refs[:3]
    tile_refs, a_refs, o_ref = refs[3 : 3 + picks], refs[3 + picks : -1], refs[-1]
    half, part = chunk // 2, rank // 2
    left = jnp.zeros((2 * rank, block), f32)
    right = jnp.zeros((2 * rank, block), f32)
    for e in range(n):
        maps = jnp.concatenate([own_ref[e], got_ref[e]])
        base = e * chunk
        left += dot(maps, dy_ref[:, base : base + half], ((1,), (1,)))
        right += dot(maps, dy_ref[:, base + half : base + chunk], ((1,), (1,)))
    own = left[:part] + right[part:rank]
    got = left[rank : rank + part] + right[rank + part :]
    first, second = jnp.where(ids[1] == 0, own, got), jnp.where(ids[1] == 0, got, own)
    total = jnp.concatenate([first, second])
    for k in range(picks):
        o_ref[k * block : (k + 1) * block, :] = tile_refs[k][0].astype(f32).astype(bf16)
        base = picks * block + rank * (1 + k)
        o_ref[base : base + rank, :] = a_refs[k][0]
    base = picks * block
    o_ref[base : base + rank, :] = (adapter_scale * total).astype(bf16)


def hidden_kernel(ids, counts, *refs, block, picks, rank):
    part_refs, side_ref, o_ref = refs[:-2], refs[-2], refs[-1]
    total = part_refs[0][0].astype(f32)
    for part_ref in part_refs[1:]:
        total = total + part_ref[0].astype(f32)
    swap = ids[0] != 0
    count = counts[ids[2]]
    low_t = jnp.zeros((rank, block), f32)
    own = slice(picks * block, picks * block + rank)
    for k in range(picks):
        first, second = total[k, :, :block], total[k, :, block:]
        gate = jnp.where(swap, second, first)
        up = jnp.where(swap, first, second)
        hidden = (gate / (1.0 + jnp.exp(-gate)) * up).astype(bf16)
        hidden = jnp.where(k < count, hidden, jnp.zeros_like(hidden))
        rows = slice(k * block, (k + 1) * block)
        pair = slice(picks * block + rank * (1 + k), picks * block + rank * (2 + k))
        dropped = hidden * side_ref[rows, :]
        low_t += dot(side_ref[pair, :], dropped, ((1,), (1,))).astype(bf16).astype(f32)
        o_ref[rows, :] = hidden
        o_ref[pair, :] = dot(side_ref[own, :], dropped).astype(bf16)
    o_ref[own, :] = low_t.astype(bf16)


def output_terms_kernel(ids, z_ref, dy_ref, o_ref, *, chunk, n):
    for s in range(n):
        part = dot(z_ref[...], dy_ref[:, s * chunk : (s + 1) * chunk])
        o_ref[s] = (adapter_scale * part).astype(bf16)


def output_kernel(ids, active, *refs, orders, block, picks, rank, runs, n):
    h_refs, (dm_ref, do_ref, b_ref, o_ref, held, stores) = refs[: len(orders)], refs[len(orders) :]
    half = dm_ref.shape[2]
    swap = ids[0] != 0
    copies = []
    for h_ref, order in zip(h_refs, orders):
        for s, q in enumerate(order):
            t = jnp.bitwise_xor(ids[2], q)
            hidden = [h_ref[s, k * block : (k + 1) * block, :] for k in range(picks)]
            hidden = jnp.concatenate(hidden, axis=1)
            sums = []
            for d_ref in (dm_ref, do_ref):
                down = jnp.concatenate([d_ref[active[t, k], :block] for k in range(picks)])
                sums.append(dot(hidden, down).astype(bf16).astype(f32))
            left = jnp.where(swap, sums[1], sums[0])
            right = jnp.where(swap, sums[0], sums[1])
            z_t = h_ref[s, picks * block : picks * block + rank, :]
            extra = adapter_scale * dot(z_t, b_ref[t * runs // n].astype(bf16), ((0,), (0,)))
            held[q, :, :half] = (left + extra[:, :half]).astype(bf16)
            held[q, :, half:] = (right + extra[:, half:]).astype(bf16)
            copy = pltpu.make_async_copy(held.at[q], o_ref.at[t], stores.at[q])
            copy.start()
            copies.append(copy)
    for copy in copies:
        copy.wait()


def join_columns_kernel(ids, c_ref, o_ref, *, chunk, n):
    for s in range(n // strips):
        o_ref[:, s * chunk : (s + 1) * chunk] = c_ref[s]


def join_copies_kernel(c_ref, o_ref, held, loads, stores, *, chunk, n):
    into = [pltpu.make_async_copy(c_ref.at[s], held.at[s], loads.at[s]) for s in range(n)]
    out = [
        pltpu.make_async_copy(held.at[s], o_ref.at[:, pl.ds(s * chunk, chunk)], stores.at[s])
        for s in range(n)
    ]
    for copy in into:
        copy.start()
    for first, second in zip(into, out):
        first.wait()
        second.start()
    for copy in out:
        copy.wait()


def gradients_kernel(ids, active, counts, *refs, orders, picks, runs, n):
    term_refs, (part_ref, ga_ref, gb_ref, sq_ref) = refs[:-4], refs[-4:]
    me = ids[2]
    per_run = n // runs
    ga_ref[...] = jnp.zeros_like(ga_ref)
    for i, order in enumerate(orders):
        for s, q in enumerate(order):
            t = jnp.bitwise_xor(me, q)
            for k in range(picks):

                @pl.when((active[t, k] == me) & (k < counts[t]))
                def _():
                    run = t * runs // n
                    ga_ref[run] = ga_ref[run] + term_refs[i * picks + k][s].astype(f32)

    for r in range(runs):
        total = part_ref[r * per_run].astype(f32)
        for q in range(1, per_run):
            total = total + part_ref[r * per_run + q].astype(f32)
        gb_ref[r] = total
        square = jnp.sum(ga_ref[r] * ga_ref[r]) + jnp.sum(total * total)
        sq_ref[r : r + 1, :] = jnp.full((1, sq_ref.shape[1]), square, f32)


def adamw_kernel(ids, *refs, limit, runs):
    sq_refs, ins, outs = refs[:-14], refs[-14:-6], refs[-6:]
    totals = sq_refs[0][...]
    for sq_ref in sq_refs[1:]:
        totals = totals + sq_ref[...]
    for r in range(runs):
        factor = jnp.minimum(1.0, limit / jnp.sqrt(totals[r : r + 1, :1]))
        for side in range(2):
            p_ref, m_ref, v_ref, g_ref = ins[4 * side : 4 * side + 4]
            grad = g_ref[r] * factor
            param = p_ref[r]
            moment = 0.9 * m_ref[r] + 0.1 * grad
            second = 0.999 * v_ref[r] + 0.001 * grad * grad
            corrected = moment / (1.0 - 0.9**10)
            spread = jnp.sqrt(second / (1.0 - 0.999**10)) + 1e-08
            outs[3 * side][r] = param - 0.01 * (corrected / spread + 0.1 * param)
            outs[3 * side + 1][r] = moment
            outs[3 * side + 2][r] = second


def body(
    tokens,
    cotangent,
    gate_weight,
    up_weight,
    down_weight,
    adapter_input_maps,
    adapter_output_maps,
    first_moment_input,
    second_moment_input,
    first_moment_output,
    second_moment_output,
    active,
    counts,
    dropout_tiles,
    seeds,
):
    hid = ("chip", "core")
    chips, cores = lax.axis_size("chip"), lax.axis_size("core")
    n = chips * cores
    core = lax.axis_index("core")
    me = lax.axis_index("chip") * cores + core
    ids = jnp.stack([lax.axis_index("groups"), core, me]).astype(jnp.int32)
    model = tokens.shape[1]
    tiles_n, block = dropout_tiles.shape[0], dropout_tiles.shape[1]
    picks = active.shape[1]
    runs, rank = adapter_output_maps.shape[0], adapter_output_maps.shape[1]
    chunk = model // n
    half = chunk // 2
    per = n // strips
    strip = model // strips
    other = [(0, 1), (1, 0)]
    across = lambda m: [(i, i ^ m) for i in range(chips)]
    sizes = dict(chunk=chunk, n=n)

    anywhere = pl.BlockSpec(memory_space=pl.ANY)
    w_send = pl.pallas_call(
        functools.partial(weight_rows_kernel, runs=runs, **sizes),
        out_shape=jax.ShapeDtypeStruct((n, chunk + rank, block), bf16),
        in_specs=[anywhere] * 3,
        out_specs=anywhere,
        scratch_shapes=[
            pltpu.VMEM((n, chunk + rank, block), bf16),
            pltpu.VMEM(adapter_input_maps.shape, f32),
            pltpu.SemaphoreType.DMA((n + 1,)),
            pltpu.SemaphoreType.DMA((n,)),
        ],
        compiler_params=pltpu.CompilerParams(vmem_limit_bytes=vmem_full),
        name="weight_rows",
    )(gate_weight, up_weight, adapter_input_maps)
    wm = lax.all_to_all(w_send, hid, split_axis=0, concat_axis=0, tiled=True)
    wo = lax.ppermute(wm, "groups", other)

    x_send = call(
        functools.partial(token_columns_kernel, **sizes),
        "token_columns",
        jax.ShapeDtypeStruct((n, block, chunk), bf16),
        (strips,),
        [pl.BlockSpec((block, strip), lambda i, ids: (0, i))],
        pl.BlockSpec((per, block, chunk), lambda i, ids: (i, 0, 0)),
        (ids,),
        (tokens,),
    )
    xb = lax.all_to_all(x_send, hid, split_axis=0, concat_axis=0, tiled=True)

    d_send = call(
        functools.partial(down_columns_kernel, block=block, rank=rank, runs=runs, **sizes),
        "down_columns",
        jax.ShapeDtypeStruct((n, block + rank, half), bf16),
        (strips,),
        [pl.BlockSpec((block, strip), lambda i, ids: (0, i)), whole(adapter_output_maps)],
        pl.BlockSpec((per, block + rank, half), lambda i, ids: (i, 0, 0)),
        (ids,),
        (down_weight, adapter_output_maps),
    )
    d_send, xb = lax.optimization_barrier((d_send, xb))
    dm = lax.all_to_all(d_send, hid, split_axis=0, concat_axis=0, tiled=True)

    products = functools.partial(partial_products, ids, active, xb, wm, wo, block, chunk)
    far = chips // 2
    (sent,) = products(0, chips, (1,))
    got = lax.ppermute(sent, "core", other)
    (kept,) = products(0, chips, (0,))
    x_kept, x_sent = pair_sums(kept, got, [(c % 2, c // 2) for c in range(chips)])
    x_got = lax.ppermute(x_sent, "chip", across(1))
    paired = pair_sums(x_kept, x_got, [(c, 0) for c in range(chips // 2)])
    summed = [paired[0]] + [
        lax.ppermute(paired[c], "chip", across(2 * c)) for c in range(1, chips // 2)
    ]
    dm, _ = lax.optimization_barrier((dm, x_got))
    do = lax.ppermute(dm, "groups", other)
    b_got = lax.ppermute(dm[:, block:], "core", other)

    rows = picks * block + rank * (1 + picks)

    def tile_spec(k):
        def at(i, ids, active, counts, seeds):
            me = ids[2]
            pick = seeds[me * runs // n] + me + 3 * active[me, k]
            return (lax.rem(pick, tiles_n), 0, 0)

        return pl.BlockSpec((1, block, block), at)

    def map_spec(k):
        return pl.BlockSpec(
            (1, rank, block), lambda i, ids, active, *_: (active[ids[2], k], chunk // rank, 0)
        )

    side = call(
        functools.partial(side_rows_kernel, block=block, picks=picks, rank=rank, **sizes),
        "side_rows",
        jax.ShapeDtypeStruct((rows, block), bf16),
        (1,),
        [
            pl.BlockSpec((n, rank, half), lambda i, *_: (0, block // rank, 0)),
            whole(b_got),
            whole(cotangent),
        ]
        + [tile_spec(k) for k in range(picks)]
        + [map_spec(k) for k in range(picks)],
        pl.BlockSpec((rows, block), lambda i, *_: (0, 0)),
        (ids, active, counts, seeds),
        (dm, b_got, cotangent) + (dropout_tiles,) * picks + (wm,) * picks,
    )
    held = call(
        functools.partial(hidden_kernel, block=block, picks=picks, rank=rank),
        "hidden_values",
        jax.ShapeDtypeStruct((rows, block), bf16),
        (1,),
        [whole(part) for part in summed] + [whole(side)],
        pl.BlockSpec((rows, block), lambda i, *_: (0, 0)),
        (ids, counts),
        (*summed, side),
    )

    term_b = call(
        functools.partial(output_terms_kernel, **sizes),
        "output_terms",
        jax.ShapeDtypeStruct((n, rank, chunk), bf16),
        (1,),
        [
            pl.BlockSpec((rank, block), lambda i, ids: (picks * block // rank, 0)),
            whole(cotangent),
        ],
        pl.BlockSpec((n, rank, chunk), lambda i, ids: (0, 0, 0)),
        (ids,),
        (held, cotangent),
    )

    near = chips // 4
    stack = jnp.stack(
        [held] + [lax.ppermute(held, "chip", across(m)) for m in (far, near, far + near)]
    )
    stack, term_b = lax.optimization_barrier((stack, term_b))
    parts_b = lax.all_to_all(term_b, hid, split_axis=0, concat_axis=0, tiled=True)
    pieces = [(stack, [0, far * cores, near * cores, (far + near) * cores])]
    mask = near // 2
    while mask:
        arrived = [
            (lax.ppermute(piece, "chip", across(mask)), [q ^ (mask * cores) for q in order])
            for piece, order in pieces
        ]
        pieces = pieces + arrived
        mask //= 2
    pieces = pieces + [
        (lax.ppermute(piece, "core", other), [q ^ 1 for q in order]) for piece, order in pieces
    ]
    gathered = [piece for piece, _ in pieces]
    orders = [order for _, order in pieces]

    at_once = lambda a: pl.BlockSpec(a.shape, lambda *_: (0,) * len(a.shape))
    out_chunks = pl.pallas_call(
        functools.partial(
            output_kernel, orders=orders, block=block, picks=picks, rank=rank, runs=runs, n=n
        ),
        out_shape=jax.ShapeDtypeStruct((n, block, chunk), bf16),
        grid_spec=pltpu.PrefetchScalarGridSpec(
            num_scalar_prefetch=2,
            grid=(1,),
            in_specs=[at_once(a) for a in (*gathered, dm, do, adapter_output_maps)],
            out_specs=anywhere,
            scratch_shapes=[
                pltpu.VMEM((n, block, chunk), bf16),
                pltpu.SemaphoreType.DMA((n,)),
            ],
        ),
        compiler_params=pltpu.CompilerParams(vmem_limit_bytes=vmem_limit),
        name="output_columns",
    )(ids, active, *gathered, dm, do, adapter_output_maps)
    out_cols = lax.all_to_all(out_chunks, hid, split_axis=0, concat_axis=0, tiled=True)
    if chunk % 128 == 0:
        output = pl.pallas_call(
            functools.partial(join_copies_kernel, **sizes),
            out_shape=jax.ShapeDtypeStruct((block, model), bf16),
            in_specs=[anywhere],
            out_specs=anywhere,
            scratch_shapes=[
                pltpu.VMEM((n, block, chunk), bf16),
                pltpu.SemaphoreType.DMA((n,)),
                pltpu.SemaphoreType.DMA((n,)),
            ],
            compiler_params=pltpu.CompilerParams(vmem_limit_bytes=vmem_full),
            name="join_columns",
        )(out_cols)
    else:
        output = call(
            functools.partial(join_columns_kernel, **sizes),
            "join_columns",
            jax.ShapeDtypeStruct((block, model), bf16),
            (strips,),
            [pl.BlockSpec((per, block, chunk), lambda i, ids: (i, 0, 0))],
            pl.BlockSpec((block, strip), lambda i, ids: (0, i)),
            (ids,),
            (out_cols,),
        )

    at_rows = lambda a, k: pl.BlockSpec(
        (a.shape[0], rank, block), lambda i, *_: (0, picks * block // rank + 1 + k, 0)
    )
    maps_a = jax.ShapeDtypeStruct(adapter_input_maps.shape, f32)
    maps_b = jax.ShapeDtypeStruct(adapter_output_maps.shape, f32)
    lanes = jax.ShapeDtypeStruct((runs, block), f32)
    grad_a, grad_b, squares = call(
        functools.partial(gradients_kernel, orders=orders, picks=picks, runs=runs, n=n),
        "gradients",
        (maps_a, maps_b, lanes),
        (1,),
        [at_rows(a, k) for a in gathered for k in range(picks)] + [whole(parts_b)],
        [whole(maps_a), whole(maps_b), whole(lanes)],
        (ids, active, counts),
        tuple(a for a in gathered for _ in range(picks)) + (parts_b,),
    )
    squares = squares + lax.ppermute(squares, "core", other)
    mask = 1
    while mask < near:
        squares = squares + lax.ppermute(squares, "chip", across(mask))
        mask *= 2
    totals = [squares] + [
        lax.ppermute(squares, "chip", across(m)) for m in (far, near, far + near)
    ]
    totals, output = lax.optimization_barrier((totals, output))
    limit = math.sqrt(rank * (n * block + model))
    updated = call(
        functools.partial(adamw_kernel, limit=limit, runs=runs),
        "adamw",
        (maps_a,) * 3 + (maps_b,) * 3,
        (1,),
        [whole(lanes)] * len(totals) + [whole(maps_a)] * 4 + [whole(maps_b)] * 4,
        [whole(maps_a)] * 3 + [whole(maps_b)] * 3,
        (ids,),
        (
            *totals,
            adapter_input_maps,
            first_moment_input,
            second_moment_input,
            grad_a,
            adapter_output_maps,
            first_moment_output,
            second_moment_output,
            grad_b,
        ),
    )
    return (output, *updated)


def solution(mesh):
    groups, n = mesh.devices.shape
    fine = Mesh(mesh.devices.reshape(groups, n // 2, 2), ("groups", "chip", "core"))
    hid = ("chip", "core")
    rows = P(("groups",) + hid, None)
    maps = P("groups", None, hid)
    return jax.shard_map(
        body,
        mesh=fine,
        in_specs=(rows, rows, P(None, hid), P(None, hid), P(hid, None))
        + (maps,) * 6
        + (P("groups", None), P("groups"), P(), P("groups")),
        out_specs=(rows,) + (maps,) * 6,
        check_vma=False,
    )
```

```python
import functools
import math

import jax
import jax.numpy as jnp
from jax import lax
from jax.experimental import pallas as pl
from jax.experimental.pallas import tpu as pltpu
from jax.sharding import Mesh, PartitionSpec as P

adapter_scale = 2.0 / 0.9
bf16 = jnp.bfloat16
f32 = jnp.float32
vmem_limit = 24 * 1024 * 1024
vmem_full = 62 * 1024 * 1024
strips = 8
paired_step = 4


def dot(a, b, dims=((1,), (0,))):
    return lax.dot_general(a, b, (dims, ((), ())), preferred_element_type=f32)


def call(kernel, name, out, grid, in_specs, out_specs, scalars, arrays, flops=0, moved=None):
    outs = out if isinstance(out, (tuple, list)) else [out]
    if moved is None:
        moved = sum(a.size * a.dtype.itemsize for a in (*arrays, *outs))
    return pl.pallas_call(
        kernel,
        out_shape=out,
        grid_spec=pltpu.PrefetchScalarGridSpec(
            num_scalar_prefetch=len(scalars),
            grid=grid,
            in_specs=in_specs,
            out_specs=out_specs,
        ),
        compiler_params=pltpu.CompilerParams(vmem_limit_bytes=vmem_limit),
        cost_estimate=pl.CostEstimate(flops=flops, bytes_accessed=moved, transcendentals=0),
        name=name,
    )(*scalars, *arrays)


def whole(a):
    zeros = (0,) * len(a.shape)
    return pl.BlockSpec(a.shape, lambda i, *_: zeros)


def weight_rows_kernel(
    gate_ref, up_ref, a_ref, o_ref, held, maps, loads, stores, *, chunk, n, runs
):
    group = lax.axis_index("groups")

    def copies(w_ref):
        return [
            pltpu.make_async_copy(
                w_ref.at[pl.ds(s * chunk, chunk)], held.at[s, pl.ds(0, chunk)], loads.at[s]
            )
            for s in range(n)
        ]

    @pl.when(group == 0)
    def _():
        for copy in copies(gate_ref):
            copy.start()

    @pl.when(group != 0)
    def _():
        for copy in copies(up_ref):
            copy.start()

    fetch = pltpu.make_async_copy(a_ref, maps, loads.at[n])
    fetch.start()
    fetch.wait()
    for s in range(n):
        held[s, chunk:, :] = maps[s * runs // n].astype(bf16)
    out = [pltpu.make_async_copy(held.at[s], o_ref.at[s], stores.at[s]) for s in range(n)]
    for s, copy in enumerate(copies(gate_ref)):
        copy.wait()
        out[s].start()
    for copy in out:
        copy.wait()


def token_columns_kernel(ids, x_ref, o_ref, *, chunk, n):
    for s in range(n // strips):
        o_ref[s] = x_ref[:, s * chunk : (s + 1) * chunk]


def down_columns_kernel(ids, d_ref, b_ref, o_ref, *, block, chunk, rank, n, runs):
    half, part = chunk // 2, rank // 2
    per = n // strips
    for s in range(per):
        base = s * chunk

        @pl.when(ids[0] == 0)
        def _():
            o_ref[s, :block, :] = d_ref[:, base : base + half]

        @pl.when(ids[0] != 0)
        def _():
            o_ref[s, :block, :] = d_ref[:, base + half : base + chunk]

        run = (pl.program_id(0) * per + s) * runs // n
        mine = b_ref[run, (s % 2) * part : (s % 2 + 1) * part, :]
        o_ref[s, block:, :] = jnp.concatenate([mine[:, :half], mine[:, half:]]).astype(bf16)


def partial_kernel(ids, active, x_ref, wm_ref, wo_ref, *o_refs, block, chunk, picks, first, sides):
    chip = ids[2] // 2
    for i in range(o_refs[0].shape[0]):
        for o_ref, side in zip(o_refs, sides):
            t = 2 * jnp.bitwise_xor(chip, first + i) + jnp.bitwise_xor(ids[1], side)
            x = x_ref[t, :block, :]
            for k in range(picks):
                j = active[t, k]
                w = jnp.concatenate([wm_ref[j, :chunk, :], wo_ref[j, :chunk, :]], axis=1)
                o_ref[i, k] = dot(x, w).astype(o_ref.dtype)


def partial_products(ids, active, xb, wm, wo, block, chunk, first, count, sides):
    n, picks = active.shape
    out = jax.ShapeDtypeStruct((count, picks, block, 2 * block), bf16)
    return call(
        functools.partial(
            partial_kernel, block=block, chunk=chunk, picks=picks, first=first, sides=sides
        ),
        "gate_up_partial",
        (out,) * len(sides),
        (1,),
        [pl.BlockSpec((n, block, chunk), lambda i, *_: (0, 0, 0)), whole(wm), whole(wo)],
        [whole(out)] * len(sides),
        (ids, active),
        (xb, wm, wo),
        flops=count * len(sides) * picks * 4 * block * block * chunk,
    )


def pair_sum_kernel(kept_ref, got_ref, *refs, places):
    o_refs, (held, stores) = refs[:-2], refs[-2:]
    copies = []
    for i, (out, at) in enumerate(places):
        held[i] = (kept_ref[i].astype(f32) + got_ref[i].astype(f32)).astype(bf16)
        copies.append(pltpu.make_async_copy(held.at[i], o_refs[out].at[at], stores.at[i]))
        copies[i].start()
    for copy in copies:
        copy.wait()


def pair_sums(kept, got, places):
    count = kept.shape[0]
    outs = 1 + max(out for out, _ in places)
    vmem = pl.BlockSpec(memory_space=pltpu.VMEM)
    return pl.pallas_call(
        functools.partial(pair_sum_kernel, places=places),
        out_shape=(jax.ShapeDtypeStruct((count // outs,) + kept.shape[1:], bf16),) * outs,
        in_specs=[vmem, vmem],
        out_specs=(pl.BlockSpec(memory_space=pltpu.HBM),) * outs,
        scratch_shapes=[pltpu.VMEM(kept.shape, bf16), pltpu.SemaphoreType.DMA((count,))],
        compiler_params=pltpu.CompilerParams(vmem_limit_bytes=vmem_limit),
        name="pair_sums",
    )(kept, got)


def side_rows_kernel(ids, active, counts, seeds, *refs, block, chunk, picks, rank, n):
    own_ref, got_ref, dy_ref = refs[:3]
    tile_refs, a_refs, o_ref = refs[3 : 3 + picks], refs[3 + picks : -1], refs[-1]
    half, part = chunk // 2, rank // 2
    left = jnp.zeros((2 * rank, block), f32)
    right = jnp.zeros((2 * rank, block), f32)
    for e in range(n):
        maps = jnp.concatenate([own_ref[e], got_ref[e]])
        base = e * chunk
        left += dot(maps, dy_ref[:, base : base + half], ((1,), (1,)))
        right += dot(maps, dy_ref[:, base + half : base + chunk], ((1,), (1,)))
    own = left[:part] + right[part:rank]
    got = left[rank : rank + part] + right[rank + part :]
    first, second = jnp.where(ids[1] == 0, own, got), jnp.where(ids[1] == 0, got, own)
    total = jnp.concatenate([first, second])
    for k in range(picks):
        o_ref[k * block : (k + 1) * block, :] = tile_refs[k][0].astype(f32).astype(bf16)
        base = picks * block + rank * (1 + k)
        o_ref[base : base + rank, :] = a_refs[k][0]
    base = picks * block
    o_ref[base : base + rank, :] = (adapter_scale * total).astype(bf16)


def hidden_kernel(ids, counts, *refs, block, picks, rank):
    part_refs, side_ref, o_ref = refs[:-2], refs[-2], refs[-1]
    total = part_refs[0][0].astype(f32)
    for part_ref in part_refs[1:]:
        total = total + part_ref[0].astype(f32)
    swap = ids[0] != 0
    count = counts[ids[2]]
    low_t = jnp.zeros((rank, block), f32)
    own = slice(picks * block, picks * block + rank)
    for k in range(picks):
        first, second = total[k, :, :block], total[k, :, block:]
        gate = jnp.where(swap, second, first)
        up = jnp.where(swap, first, second)
        hidden = (gate / (1.0 + jnp.exp(-gate)) * up).astype(bf16)
        hidden = jnp.where(k < count, hidden, jnp.zeros_like(hidden))
        rows = slice(k * block, (k + 1) * block)
        pair = slice(picks * block + rank * (1 + k), picks * block + rank * (2 + k))
        dropped = hidden * side_ref[rows, :]
        low_t += dot(side_ref[pair, :], dropped, ((1,), (1,))).astype(bf16).astype(f32)
        o_ref[rows, :] = hidden
    o_ref[own, :] = low_t.astype(bf16)
    o_ref[picks * block + rank :, :] = side_ref[own, :]


def output_terms_kernel(ids, z_ref, dy_ref, o_ref, *, chunk, n):
    for s in range(n):
        part = dot(z_ref[...], dy_ref[:, s * chunk : (s + 1) * chunk])
        o_ref[s] = (adapter_scale * part).astype(bf16)


def output_kernel(ids, active, *refs, orders, block, picks, rank, runs, n):
    h_refs, (dm_ref, do_ref, b_ref, o_ref, held, stores) = refs[: len(orders)], refs[len(orders) :]
    half = dm_ref.shape[2]
    swap = ids[0] != 0
    copies = []
    for h_ref, order in zip(h_refs, orders):
        for s, q in enumerate(order):
            t = jnp.bitwise_xor(ids[2], q)
            hidden = [h_ref[s, k * block : (k + 1) * block, :] for k in range(picks)]
            hidden = jnp.concatenate(hidden, axis=1)
            sums = []
            for d_ref in (dm_ref, do_ref):
                down = jnp.concatenate([d_ref[active[t, k], :block] for k in range(picks)])
                sums.append(dot(hidden, down).astype(bf16).astype(f32))
            left = jnp.where(swap, sums[1], sums[0])
            right = jnp.where(swap, sums[0], sums[1])
            z_t = h_ref[s, picks * block : picks * block + rank, :]
            extra = adapter_scale * dot(z_t, b_ref[t * runs // n].astype(bf16), ((0,), (0,)))
            held[q, :, :half] = (left + extra[:, :half]).astype(bf16)
            held[q, :, half:] = (right + extra[:, half:]).astype(bf16)
            copy = pltpu.make_async_copy(held.at[q], o_ref.at[t], stores.at[q])
            copy.start()
            copies.append(copy)
    for copy in copies:
        copy.wait()


def join_columns_kernel(ids, c_ref, o_ref, *, chunk, n):
    for s in range(n // strips):
        o_ref[:, s * chunk : (s + 1) * chunk] = c_ref[s]


def join_copies_kernel(c_ref, o_ref, stores, *, chunk, n):
    copies = [
        pltpu.make_async_copy(c_ref.at[s], o_ref.at[:, pl.ds(s * chunk, chunk)], stores.at[s])
        for s in range(n)
    ]
    for copy in copies:
        copy.start()
    for copy in copies:
        copy.wait()


def gradients_kernel(ids, active, counts, seeds, order, *refs, sizes, block, picks, rank, runs, n):
    h_refs, (tile_ref, part_ref, ga_ref, gb_ref, sq_ref) = refs[:-5], refs[-5:]
    me = ids[2]
    per_run = n // runs
    ga_ref[...] = jnp.zeros_like(ga_ref)

    def add(h_ref, base, s, carry):
        t = jnp.bitwise_xor(me, order[base + s])
        run = lax.div(t * runs, n)
        tile = lax.rem(seeds[run] + t + 3 * me, tile_ref.shape[0])
        for k in range(picks):

            @pl.when((active[t, k] == me) & (k < counts[t]))
            def _():
                kept = tile_ref[tile].astype(f32).astype(bf16)
                dropped = h_ref[s, k * block : (k + 1) * block, :] * kept
                dz_t = h_ref[s, picks * block + rank : picks * block + 2 * rank, :]
                ga_ref[run] = ga_ref[run] + dot(dz_t, dropped)

        return carry

    base = 0
    for h_ref, size in zip(h_refs, sizes):
        lax.fori_loop(0, size, functools.partial(add, h_ref, base), 0)
        base += size
    for r in range(runs):
        total = part_ref[r * per_run].astype(f32)
        for q in range(1, per_run):
            total = total + part_ref[r * per_run + q].astype(f32)
        gb_ref[r] = total
        square = jnp.sum(ga_ref[r] * ga_ref[r]) + jnp.sum(total * total)
        sq_ref[r : r + 1, :] = jnp.full((1, sq_ref.shape[1]), square, f32)


def adamw_kernel(ids, *refs, limit, runs):
    sq_refs, ins, outs = refs[:-14], refs[-14:-6], refs[-6:]
    totals = sq_refs[0][...]
    for sq_ref in sq_refs[1:]:
        totals = totals + sq_ref[...]
    for r in range(runs):
        factor = jnp.minimum(1.0, limit / jnp.sqrt(totals[r : r + 1, :1]))
        for side in range(2):
            p_ref, m_ref, v_ref, g_ref = ins[4 * side : 4 * side + 4]
            grad = g_ref[r] * factor
            param = p_ref[r]
            moment = 0.9 * m_ref[r] + 0.1 * grad
            second = 0.999 * v_ref[r] + 0.001 * grad * grad
            corrected = moment / (1.0 - 0.9**10)
            spread = jnp.sqrt(second / (1.0 - 0.999**10)) + 1e-08
            outs[3 * side][r] = param - 0.01 * (corrected / spread + 0.1 * param)
            outs[3 * side + 1][r] = moment
            outs[3 * side + 2][r] = second


def body(
    tokens,
    cotangent,
    gate_weight,
    up_weight,
    down_weight,
    adapter_input_maps,
    adapter_output_maps,
    first_moment_input,
    second_moment_input,
    first_moment_output,
    second_moment_output,
    active,
    counts,
    dropout_tiles,
    seeds,
):
    hid = ("chip", "core")
    chips, cores = lax.axis_size("chip"), lax.axis_size("core")
    n = chips * cores
    core = lax.axis_index("core")
    me = lax.axis_index("chip") * cores + core
    ids = jnp.stack([lax.axis_index("groups"), core, me]).astype(jnp.int32)
    model = tokens.shape[1]
    tiles_n, block = dropout_tiles.shape[0], dropout_tiles.shape[1]
    picks = active.shape[1]
    runs, rank = adapter_output_maps.shape[0], adapter_output_maps.shape[1]
    chunk = model // n
    half = chunk // 2
    per = n // strips
    strip = model // strips
    other = [(0, 1), (1, 0)]
    across = lambda m: [(i, i ^ m) for i in range(chips)]
    sizes = dict(chunk=chunk, n=n)

    anywhere = pl.BlockSpec(memory_space=pl.ANY)
    vmem = pl.BlockSpec(memory_space=pltpu.VMEM)
    w_send = pl.pallas_call(
        functools.partial(weight_rows_kernel, runs=runs, **sizes),
        out_shape=jax.ShapeDtypeStruct((n, chunk + rank, block), bf16),
        in_specs=[anywhere] * 3,
        out_specs=anywhere,
        scratch_shapes=[
            pltpu.VMEM((n, chunk + rank, block), bf16),
            pltpu.VMEM(adapter_input_maps.shape, f32),
            pltpu.SemaphoreType.DMA((n + 1,)),
            pltpu.SemaphoreType.DMA((n,)),
        ],
        compiler_params=pltpu.CompilerParams(vmem_limit_bytes=vmem_full),
        name="weight_rows",
    )(gate_weight, up_weight, adapter_input_maps)
    wm = lax.all_to_all(w_send, hid, split_axis=0, concat_axis=0, tiled=True)
    wo = lax.ppermute(wm, "groups", other)

    x_send = call(
        functools.partial(token_columns_kernel, **sizes),
        "token_columns",
        jax.ShapeDtypeStruct((n, block, chunk), bf16),
        (strips,),
        [pl.BlockSpec((block, strip), lambda i, ids: (0, i))],
        pl.BlockSpec((per, block, chunk), lambda i, ids: (i, 0, 0)),
        (ids,),
        (tokens,),
    )
    xb = lax.all_to_all(x_send, hid, split_axis=0, concat_axis=0, tiled=True)

    d_send = call(
        functools.partial(down_columns_kernel, block=block, rank=rank, runs=runs, **sizes),
        "down_columns",
        jax.ShapeDtypeStruct((n, block + rank, half), bf16),
        (strips,),
        [pl.BlockSpec((block, strip), lambda i, ids: (0, i)), whole(adapter_output_maps)],
        pl.BlockSpec((per, block + rank, half), lambda i, ids: (i, 0, 0)),
        (ids,),
        (down_weight, adapter_output_maps),
    )
    d_send, xb = lax.optimization_barrier((d_send, xb))
    dm = lax.all_to_all(d_send, hid, split_axis=0, concat_axis=0, tiled=True)

    products = functools.partial(partial_products, ids, active, xb, wm, wo, block, chunk)
    far = chips // 2
    (sent,) = products(0, chips, (1,))
    got = lax.ppermute(sent, "core", other)
    (kept,) = products(0, chips, (0,))
    x_kept, x_sent = pair_sums(kept, got, [(c % 2, c // 2) for c in range(chips)])
    x_got = lax.ppermute(x_sent, "chip", across(1))
    paired = pair_sums(x_kept, x_got, [(c, 0) for c in range(chips // 2)])
    summed = [paired[0]] + [
        lax.ppermute(paired[c], "chip", across(2 * c)) for c in range(1, chips // 2)
    ]
    dm, _ = lax.optimization_barrier((dm, x_got))
    do = lax.ppermute(dm, "groups", other)
    b_got = lax.ppermute(dm[:, block:], "core", other)

    rows = picks * block + rank * (1 + picks)
    kept_rows = picks * block + 2 * rank

    def tile_spec(k):
        def at(i, ids, active, counts, seeds):
            me = ids[2]
            pick = seeds[me * runs // n] + me + 3 * active[me, k]
            return (lax.rem(pick, tiles_n), 0, 0)

        return pl.BlockSpec((1, block, block), at)

    def map_spec(k):
        return pl.BlockSpec(
            (1, rank, block), lambda i, ids, active, *_: (active[ids[2], k], chunk // rank, 0)
        )

    side = call(
        functools.partial(side_rows_kernel, block=block, picks=picks, rank=rank, **sizes),
        "side_rows",
        jax.ShapeDtypeStruct((rows, block), bf16),
        (1,),
        [
            pl.BlockSpec((n, rank, half), lambda i, *_: (0, block // rank, 0)),
            whole(b_got),
            whole(cotangent),
        ]
        + [tile_spec(k) for k in range(picks)]
        + [map_spec(k) for k in range(picks)],
        pl.BlockSpec((rows, block), lambda i, *_: (0, 0)),
        (ids, active, counts, seeds),
        (dm, b_got, cotangent) + (dropout_tiles,) * picks + (wm,) * picks,
    )
    held = call(
        functools.partial(hidden_kernel, block=block, picks=picks, rank=rank),
        "hidden_values",
        jax.ShapeDtypeStruct((kept_rows, block), bf16),
        (1,),
        [whole(part) for part in summed] + [whole(side)],
        pl.BlockSpec((kept_rows, block), lambda i, *_: (0, 0)),
        (ids, counts),
        (*summed, side),
    )

    term_b = call(
        functools.partial(output_terms_kernel, **sizes),
        "output_terms",
        jax.ShapeDtypeStruct((n, rank, chunk), bf16),
        (1,),
        [
            pl.BlockSpec((rank, block), lambda i, ids: (picks * block // rank, 0)),
            whole(cotangent),
        ],
        pl.BlockSpec((n, rank, chunk), lambda i, ids: (0, 0, 0)),
        (ids,),
        (held, cotangent),
    )

    near = chips // 4
    stack = jnp.stack(
        [held] + [lax.ppermute(held, "chip", across(m)) for m in (far, near, far + near)]
    )
    stack, _ = lax.optimization_barrier((stack, term_b))
    parts_b = lax.all_to_all(term_b, hid, split_axis=0, concat_axis=0, tiled=True)
    pieces = [(stack, [0, far * cores, near * cores, (far + near) * cores])]
    mask = near // 2
    while mask:
        arrived = [
            (lax.ppermute(piece, "chip", across(mask)), [q ^ (mask * cores) for q in order])
            for piece, order in pieces
        ]
        pieces = pieces + arrived
        mask //= 2
    pieces = pieces + [
        (lax.ppermute(piece, "core", other), [q ^ 1 for q in order]) for piece, order in pieces
    ]
    gathered = [piece for piece, _ in pieces]
    orders = [order for _, order in pieces]

    out_chunks = pl.pallas_call(
        functools.partial(
            output_kernel, orders=orders, block=block, picks=picks, rank=rank, runs=runs, n=n
        ),
        out_shape=jax.ShapeDtypeStruct((n, block, chunk), bf16),
        in_specs=[pl.BlockSpec(memory_space=pltpu.SMEM)] * 2 + [vmem] * (len(gathered) + 3),
        out_specs=anywhere,
        scratch_shapes=[
            pltpu.VMEM((n, block, chunk), bf16),
            pltpu.SemaphoreType.DMA((n,)),
        ],
        compiler_params=pltpu.CompilerParams(vmem_limit_bytes=vmem_limit),
        name="output_columns",
    )(ids, active, *gathered, dm, do, adapter_output_maps)
    out_cols = lax.all_to_all(out_chunks, hid, split_axis=0, concat_axis=0, tiled=True)
    if chunk % 128 == 0:
        output = pl.pallas_call(
            functools.partial(join_copies_kernel, **sizes),
            out_shape=jax.ShapeDtypeStruct((block, model), bf16),
            in_specs=[vmem],
            out_specs=anywhere,
            scratch_shapes=[pltpu.SemaphoreType.DMA((n,))],
            compiler_params=pltpu.CompilerParams(vmem_limit_bytes=8 * 1024 * 1024),
            name="join_columns",
        )(out_cols)
    else:
        output = call(
            functools.partial(join_columns_kernel, **sizes),
            "join_columns",
            jax.ShapeDtypeStruct((block, model), bf16),
            (strips,),
            [pl.BlockSpec((per, block, chunk), lambda i, ids: (i, 0, 0))],
            pl.BlockSpec((block, strip), lambda i, ids: (0, i)),
            (ids,),
            (out_cols,),
        )

    maps_a = jax.ShapeDtypeStruct(adapter_input_maps.shape, f32)
    maps_b = jax.ShapeDtypeStruct(adapter_output_maps.shape, f32)
    lanes = jax.ShapeDtypeStruct((runs, block), f32)
    grad_a, grad_b, squares = call(
        functools.partial(
            gradients_kernel,
            sizes=[len(order) for order in orders],
            block=block,
            picks=picks,
            rank=rank,
            runs=runs,
            n=n,
        ),
        "gradients",
        (maps_a, maps_b, lanes),
        (1,),
        [whole(a) for a in (*gathered, dropout_tiles, parts_b)],
        [whole(maps_a), whole(maps_b), whole(lanes)],
        (ids, active, counts, seeds, jnp.array(sum(orders, []), jnp.int32)),
        (*gathered, dropout_tiles, parts_b),
    )
    squares = squares + lax.ppermute(squares, "core", other)
    mask = 1
    while mask < near:
        squares = squares + lax.ppermute(squares, "chip", across(mask))
        mask *= 2
    totals = [squares] + [
        lax.ppermute(squares, "chip", across(m)) for m in (far, near, far + near)
    ]
    totals, output = lax.optimization_barrier((totals, output))
    limit = math.sqrt(rank * (n * block + model))
    updated = call(
        functools.partial(adamw_kernel, limit=limit, runs=runs),
        "adamw",
        (maps_a,) * 3 + (maps_b,) * 3,
        (1,),
        [whole(lanes)] * len(totals) + [whole(maps_a)] * 4 + [whole(maps_b)] * 4,
        [whole(maps_a)] * 3 + [whole(maps_b)] * 3,
        (ids,),
        (
            *totals,
            adapter_input_maps,
            first_moment_input,
            second_moment_input,
            grad_a,
            adapter_output_maps,
            first_moment_output,
            second_moment_output,
            grad_b,
        ),
    )
    return (output, *updated)


def solution(mesh):
    groups, n = mesh.devices.shape
    fine = Mesh(mesh.devices.reshape(groups, n // 2, 2), ("groups", "chip", "core"))
    hid = ("chip", "core")
    rows = P(("groups",) + hid, None)
    maps = P("groups", None, hid)
    return jax.shard_map(
        body,
        mesh=fine,
        in_specs=(rows, rows, P(None, hid), P(None, hid), P(hid, None))
        + (maps,) * 6
        + (P("groups", None), P("groups"), P(), P("groups")),
        out_specs=(rows,) + (maps,) * 6,
        check_vma=False,
    )
```

```python
import functools
import math

import jax
import jax.numpy as jnp
from jax import lax
from jax.experimental import pallas as pl
from jax.experimental.pallas import tpu as pltpu
from jax.sharding import Mesh, PartitionSpec as P

adapter_scale = 2.0 / 0.9
bf16 = jnp.bfloat16
f32 = jnp.float32
vmem_limit = 24 * 1024 * 1024
vmem_full = 62 * 1024 * 1024
strips = 8
paired_step = 4


def dot(a, b, dims=((1,), (0,))):
    return lax.dot_general(a, b, (dims, ((), ())), preferred_element_type=f32)


def call(kernel, name, out, grid, in_specs, out_specs, scalars, arrays, flops=0, moved=None):
    outs = out if isinstance(out, (tuple, list)) else [out]
    if moved is None:
        moved = sum(a.size * a.dtype.itemsize for a in (*arrays, *outs))
    return pl.pallas_call(
        kernel,
        out_shape=out,
        grid_spec=pltpu.PrefetchScalarGridSpec(
            num_scalar_prefetch=len(scalars),
            grid=grid,
            in_specs=in_specs,
            out_specs=out_specs,
        ),
        compiler_params=pltpu.CompilerParams(vmem_limit_bytes=vmem_limit),
        cost_estimate=pl.CostEstimate(flops=flops, bytes_accessed=moved, transcendentals=0),
        name=name,
    )(*scalars, *arrays)


def whole(a):
    zeros = (0,) * len(a.shape)
    return pl.BlockSpec(a.shape, lambda i, *_: zeros)


def weight_rows_kernel(
    gate_ref, up_ref, a_ref, o_ref, held, maps, loads, stores, *, chunk, n, runs
):
    group = lax.axis_index("groups")

    def copies(w_ref):
        return [
            pltpu.make_async_copy(
                w_ref.at[pl.ds(s * chunk, chunk)], held.at[s, pl.ds(0, chunk)], loads.at[s]
            )
            for s in range(n)
        ]

    @pl.when(group == 0)
    def _():
        for copy in copies(gate_ref):
            copy.start()

    @pl.when(group != 0)
    def _():
        for copy in copies(up_ref):
            copy.start()

    fetch = pltpu.make_async_copy(a_ref, maps, loads.at[n])
    fetch.start()
    fetch.wait()
    for s in range(n):
        held[s, chunk:, :] = maps[s * runs // n].astype(bf16)
    out = [pltpu.make_async_copy(held.at[s], o_ref.at[s], stores.at[s]) for s in range(n)]
    for s, copy in enumerate(copies(gate_ref)):
        copy.wait()
        out[s].start()
    for copy in out:
        copy.wait()


def token_columns_kernel(ids, x_ref, o_ref, *, chunk, n):
    for s in range(n // strips):
        o_ref[s] = x_ref[:, s * chunk : (s + 1) * chunk]


def down_columns_kernel(ids, d_ref, b_ref, o_ref, *, block, chunk, rank, n, runs):
    half, part = chunk // 2, rank // 2
    per = n // strips
    for s in range(per):
        base = s * chunk

        @pl.when(ids[0] == 0)
        def _():
            o_ref[s, :block, :] = d_ref[:, base : base + half]

        @pl.when(ids[0] != 0)
        def _():
            o_ref[s, :block, :] = d_ref[:, base + half : base + chunk]

        run = (pl.program_id(0) * per + s) * runs // n
        mine = b_ref[run, (s % 2) * part : (s % 2 + 1) * part, :]
        o_ref[s, block:, :] = jnp.concatenate([mine[:, :half], mine[:, half:]]).astype(bf16)


def partial_kernel(ids, active, x_ref, wm_ref, wo_ref, *o_refs, block, chunk, picks, first, sides):
    chip = ids[2] // 2
    for i in range(o_refs[0].shape[0]):
        for o_ref, side in zip(o_refs, sides):
            t = 2 * jnp.bitwise_xor(chip, first + i) + jnp.bitwise_xor(ids[1], side)
            x = x_ref[t, :block, :]
            for k in range(picks):
                j = active[t, k]
                w = jnp.concatenate([wm_ref[j, :chunk, :], wo_ref[j, :chunk, :]], axis=1)
                o_ref[i, k] = dot(x, w).astype(o_ref.dtype)


def partial_products(ids, active, xb, wm, wo, block, chunk, first, count, sides):
    n, picks = active.shape
    out = jax.ShapeDtypeStruct((count, picks, block, 2 * block), bf16)
    return call(
        functools.partial(
            partial_kernel, block=block, chunk=chunk, picks=picks, first=first, sides=sides
        ),
        "gate_up_partial",
        (out,) * len(sides),
        (1,),
        [pl.BlockSpec((n, block, chunk), lambda i, *_: (0, 0, 0)), whole(wm), whole(wo)],
        [whole(out)] * len(sides),
        (ids, active),
        (xb, wm, wo),
        flops=count * len(sides) * picks * 4 * block * block * chunk,
    )


def pair_sum_kernel(kept_ref, got_ref, *refs, places):
    o_refs, (held, stores) = refs[:-2], refs[-2:]
    copies = []
    for i, (out, at) in enumerate(places):
        held[i] = (kept_ref[i].astype(f32) + got_ref[i].astype(f32)).astype(bf16)
        copies.append(pltpu.make_async_copy(held.at[i], o_refs[out].at[at], stores.at[i]))
        copies[i].start()
    for copy in copies:
        copy.wait()


def pair_sums(kept, got, places):
    count = kept.shape[0]
    outs = 1 + max(out for out, _ in places)
    vmem = pl.BlockSpec(memory_space=pltpu.VMEM)
    return pl.pallas_call(
        functools.partial(pair_sum_kernel, places=places),
        out_shape=(jax.ShapeDtypeStruct((count // outs,) + kept.shape[1:], bf16),) * outs,
        in_specs=[vmem, vmem],
        out_specs=(pl.BlockSpec(memory_space=pltpu.HBM),) * outs,
        scratch_shapes=[pltpu.VMEM(kept.shape, bf16), pltpu.SemaphoreType.DMA((count,))],
        compiler_params=pltpu.CompilerParams(vmem_limit_bytes=vmem_limit),
        name="pair_sums",
    )(kept, got)


def side_rows_kernel(ids, active, counts, seeds, *refs, block, chunk, picks, rank, n):
    own_ref, got_ref, dy_ref = refs[:3]
    tile_refs, a_refs, o_ref = refs[3 : 3 + picks], refs[3 + picks : -1], refs[-1]
    half, part = chunk // 2, rank // 2
    left = jnp.zeros((2 * rank, block), f32)
    right = jnp.zeros((2 * rank, block), f32)
    for e in range(n):
        maps = jnp.concatenate([own_ref[e], got_ref[e]])
        base = e * chunk
        left += dot(maps, dy_ref[:, base : base + half], ((1,), (1,)))
        right += dot(maps, dy_ref[:, base + half : base + chunk], ((1,), (1,)))
    own = left[:part] + right[part:rank]
    got = left[rank : rank + part] + right[rank + part :]
    first, second = jnp.where(ids[1] == 0, own, got), jnp.where(ids[1] == 0, got, own)
    total = jnp.concatenate([first, second])
    for k in range(picks):
        o_ref[k * block : (k + 1) * block, :] = tile_refs[k][0].astype(f32).astype(bf16)
        base = picks * block + rank * (1 + k)
        o_ref[base : base + rank, :] = a_refs[k][0]
    base = picks * block
    o_ref[base : base + rank, :] = (adapter_scale * total).astype(bf16)


def hidden_kernel(ids, counts, *refs, block, picks, rank):
    part_refs, side_ref, o_ref = refs[:-2], refs[-2], refs[-1]
    total = part_refs[0][0].astype(f32)
    for part_ref in part_refs[1:]:
        total = total + part_ref[0].astype(f32)
    swap = ids[0] != 0
    count = counts[ids[2]]
    low_t = jnp.zeros((rank, block), f32)
    own = slice(picks * block, picks * block + rank)
    for k in range(picks):
        first, second = total[k, :, :block], total[k, :, block:]
        gate = jnp.where(swap, second, first)
        up = jnp.where(swap, first, second)
        hidden = (gate / (1.0 + jnp.exp(-gate)) * up).astype(bf16)
        hidden = jnp.where(k < count, hidden, jnp.zeros_like(hidden))
        rows = slice(k * block, (k + 1) * block)
        pair = slice(picks * block + rank * (1 + k), picks * block + rank * (2 + k))
        dropped = hidden * side_ref[rows, :]
        low_t += dot(side_ref[pair, :], dropped, ((1,), (1,))).astype(bf16).astype(f32)
        o_ref[rows, :] = hidden
    o_ref[own, :] = low_t.astype(bf16)
    o_ref[picks * block + rank :, :] = side_ref[own, :]


def output_terms_kernel(ids, z_ref, dy_ref, o_ref, *, chunk, n):
    for s in range(n):
        part = dot(z_ref[...], dy_ref[:, s * chunk : (s + 1) * chunk])
        o_ref[s] = (adapter_scale * part).astype(bf16)


def output_kernel(ids, active, *refs, orders, block, picks, rank, runs, n):
    h_refs, (dm_ref, do_ref, b_ref, o_ref, held, stores) = refs[: len(orders)], refs[len(orders) :]
    half = dm_ref.shape[2]
    swap = ids[0] != 0
    copies = []
    for h_ref, order in zip(h_refs, orders):
        for s, q in enumerate(order):
            t = jnp.bitwise_xor(ids[2], q)
            hidden = [h_ref[s, k * block : (k + 1) * block, :] for k in range(picks)]
            hidden = jnp.concatenate(hidden, axis=1)
            sums = []
            for d_ref in (dm_ref, do_ref):
                down = jnp.concatenate([d_ref[active[t, k], :block] for k in range(picks)])
                sums.append(dot(hidden, down).astype(bf16).astype(f32))
            left = jnp.where(swap, sums[1], sums[0])
            right = jnp.where(swap, sums[0], sums[1])
            z_t = h_ref[s, picks * block : picks * block + rank, :]
            extra = adapter_scale * dot(z_t, b_ref[t * runs // n].astype(bf16), ((0,), (0,)))
            held[q, :, :half] = (left + extra[:, :half]).astype(bf16)
            held[q, :, half:] = (right + extra[:, half:]).astype(bf16)
            copy = pltpu.make_async_copy(held.at[q], o_ref.at[t], stores.at[q])
            copy.start()
            copies.append(copy)
    for copy in copies:
        copy.wait()


def join_columns_kernel(ids, c_ref, o_ref, *, chunk, n):
    for s in range(n // strips):
        o_ref[:, s * chunk : (s + 1) * chunk] = c_ref[s]


def join_copies_kernel(c_ref, o_ref, stores, *, chunk, n):
    copies = [
        pltpu.make_async_copy(c_ref.at[s], o_ref.at[:, pl.ds(s * chunk, chunk)], stores.at[s])
        for s in range(n)
    ]
    for copy in copies:
        copy.start()
    for copy in copies:
        copy.wait()


def gradients_kernel(ids, active, counts, seeds, order, *refs, sizes, block, picks, rank, runs, n):
    h_refs, (tile_ref, part_ref, ga_ref, gb_ref, sq_ref) = refs[:-5], refs[-5:]
    me = ids[2]
    per_run = n // runs
    ga_ref[...] = jnp.zeros_like(ga_ref)

    def add(h_ref, base, s, carry):
        t = jnp.bitwise_xor(me, order[base + s])
        run = lax.div(t * runs, n)
        tile = lax.rem(seeds[run] + t + 3 * me, tile_ref.shape[0])
        for k in range(picks):

            @pl.when((active[t, k] == me) & (k < counts[t]))
            def _():
                kept = tile_ref[tile].astype(f32).astype(bf16)
                dropped = h_ref[s, k * block : (k + 1) * block, :] * kept
                dz_t = h_ref[s, picks * block + rank : picks * block + 2 * rank, :]
                ga_ref[run] = ga_ref[run] + dot(dz_t, dropped)

        return carry

    base = 0
    for h_ref, size in zip(h_refs, sizes):
        lax.fori_loop(0, size, functools.partial(add, h_ref, base), 0)
        base += size
    for r in range(runs):
        total = part_ref[r * per_run].astype(f32)
        for q in range(1, per_run):
            total = total + part_ref[r * per_run + q].astype(f32)
        gb_ref[r] = total
        square = jnp.sum(ga_ref[r] * ga_ref[r]) + jnp.sum(total * total)
        sq_ref[r : r + 1, :] = jnp.full((1, sq_ref.shape[1]), square, f32)


def adamw_kernel(ids, *refs, limit, runs):
    sq_refs, ins, outs = refs[:-14], refs[-14:-6], refs[-6:]
    totals = sq_refs[0][...]
    for sq_ref in sq_refs[1:]:
        totals = totals + sq_ref[...]
    for r in range(runs):
        factor = jnp.minimum(1.0, limit / jnp.sqrt(totals[r : r + 1, :1]))
        for side in range(2):
            p_ref, m_ref, v_ref, g_ref = ins[4 * side : 4 * side + 4]
            grad = g_ref[r] * factor
            param = p_ref[r]
            moment = 0.9 * m_ref[r] + 0.1 * grad
            second = 0.999 * v_ref[r] + 0.001 * grad * grad
            corrected = moment / (1.0 - 0.9**10)
            spread = jnp.sqrt(second / (1.0 - 0.999**10)) + 1e-08
            outs[3 * side][r] = param - 0.01 * (corrected / spread + 0.1 * param)
            outs[3 * side + 1][r] = moment
            outs[3 * side + 2][r] = second


def body(
    tokens,
    cotangent,
    gate_weight,
    up_weight,
    down_weight,
    adapter_input_maps,
    adapter_output_maps,
    first_moment_input,
    second_moment_input,
    first_moment_output,
    second_moment_output,
    active,
    counts,
    dropout_tiles,
    seeds,
):
    hid = ("chip", "core")
    chips, cores = lax.axis_size("chip"), lax.axis_size("core")
    n = chips * cores
    core = lax.axis_index("core")
    me = lax.axis_index("chip") * cores + core
    ids = jnp.stack([lax.axis_index("groups"), core, me]).astype(jnp.int32)
    model = tokens.shape[1]
    tiles_n, block = dropout_tiles.shape[0], dropout_tiles.shape[1]
    picks = active.shape[1]
    runs, rank = adapter_output_maps.shape[0], adapter_output_maps.shape[1]
    chunk = model // n
    half = chunk // 2
    per = n // strips
    strip = model // strips
    other = [(0, 1), (1, 0)]
    across = lambda m: [(i, i ^ m) for i in range(chips)]
    sizes = dict(chunk=chunk, n=n)

    anywhere = pl.BlockSpec(memory_space=pl.ANY)
    vmem = pl.BlockSpec(memory_space=pltpu.VMEM)
    w_send = pl.pallas_call(
        functools.partial(weight_rows_kernel, runs=runs, **sizes),
        out_shape=jax.ShapeDtypeStruct((n, chunk + rank, block), bf16),
        in_specs=[anywhere] * 3,
        out_specs=anywhere,
        scratch_shapes=[
            pltpu.VMEM((n, chunk + rank, block), bf16),
            pltpu.VMEM(adapter_input_maps.shape, f32),
            pltpu.SemaphoreType.DMA((n + 1,)),
            pltpu.SemaphoreType.DMA((n,)),
        ],
        compiler_params=pltpu.CompilerParams(vmem_limit_bytes=vmem_full),
        name="weight_rows",
    )(gate_weight, up_weight, adapter_input_maps)
    wm = lax.all_to_all(w_send, hid, split_axis=0, concat_axis=0, tiled=True)
    wo = lax.ppermute(wm, "groups", other)

    x_send = call(
        functools.partial(token_columns_kernel, **sizes),
        "token_columns",
        jax.ShapeDtypeStruct((n, block, chunk), bf16),
        (strips,),
        [pl.BlockSpec((block, strip), lambda i, ids: (0, i))],
        pl.BlockSpec((per, block, chunk), lambda i, ids: (i, 0, 0)),
        (ids,),
        (tokens,),
    )
    xb = lax.all_to_all(x_send, hid, split_axis=0, concat_axis=0, tiled=True)

    d_send = call(
        functools.partial(down_columns_kernel, block=block, rank=rank, runs=runs, **sizes),
        "down_columns",
        jax.ShapeDtypeStruct((n, block + rank, half), bf16),
        (strips,),
        [pl.BlockSpec((block, strip), lambda i, ids: (0, i)), whole(adapter_output_maps)],
        pl.BlockSpec((per, block + rank, half), lambda i, ids: (i, 0, 0)),
        (ids,),
        (down_weight, adapter_output_maps),
    )
    d_send, xb = lax.optimization_barrier((d_send, xb))
    dm = lax.all_to_all(d_send, hid, split_axis=0, concat_axis=0, tiled=True)

    products = functools.partial(partial_products, ids, active, xb, wm, wo, block, chunk)
    far = chips // 2
    (sent,) = products(0, chips, (1,))
    got = lax.ppermute(sent, "core", other)
    (kept,) = products(0, chips, (0,))
    x_kept, x_sent = pair_sums(kept, got, [(c % 2, c // 2) for c in range(chips)])
    x_got = lax.ppermute(x_sent, "chip", across(1))
    paired = pair_sums(x_kept, x_got, [(c, 0) for c in range(chips // 2)])
    summed = [paired[0]] + [
        lax.ppermute(paired[c], "chip", across(2 * c)) for c in range(1, chips // 2)
    ]
    dm, _ = lax.optimization_barrier((dm, x_sent))
    do = lax.ppermute(dm, "groups", other)
    b_got = lax.ppermute(dm[:, block:], "core", other)

    rows = picks * block + rank * (1 + picks)
    kept_rows = picks * block + 2 * rank

    def tile_spec(k):
        def at(i, ids, active, counts, seeds):
            me = ids[2]
            pick = seeds[me * runs // n] + me + 3 * active[me, k]
            return (lax.rem(pick, tiles_n), 0, 0)

        return pl.BlockSpec((1, block, block), at)

    def map_spec(k):
        return pl.BlockSpec(
            (1, rank, block), lambda i, ids, active, *_: (active[ids[2], k], chunk // rank, 0)
        )

    side = call(
        functools.partial(side_rows_kernel, block=block, picks=picks, rank=rank, **sizes),
        "side_rows",
        jax.ShapeDtypeStruct((rows, block), bf16),
        (1,),
        [
            pl.BlockSpec((n, rank, half), lambda i, *_: (0, block // rank, 0)),
            whole(b_got),
            whole(cotangent),
        ]
        + [tile_spec(k) for k in range(picks)]
        + [map_spec(k) for k in range(picks)],
        pl.BlockSpec((rows, block), lambda i, *_: (0, 0)),
        (ids, active, counts, seeds),
        (dm, b_got, cotangent) + (dropout_tiles,) * picks + (wm,) * picks,
    )
    held = call(
        functools.partial(hidden_kernel, block=block, picks=picks, rank=rank),
        "hidden_values",
        jax.ShapeDtypeStruct((kept_rows, block), bf16),
        (1,),
        [whole(part) for part in summed] + [whole(side)],
        pl.BlockSpec((kept_rows, block), lambda i, *_: (0, 0)),
        (ids, counts),
        (*summed, side),
    )

    term_b = call(
        functools.partial(output_terms_kernel, **sizes),
        "output_terms",
        jax.ShapeDtypeStruct((n, rank, chunk), bf16),
        (1,),
        [
            pl.BlockSpec((rank, block), lambda i, ids: (picks * block // rank, 0)),
            whole(cotangent),
        ],
        pl.BlockSpec((n, rank, chunk), lambda i, ids: (0, 0, 0)),
        (ids,),
        (held, cotangent),
    )

    near = chips // 4
    stack = jnp.stack(
        [held] + [lax.ppermute(held, "chip", across(m)) for m in (near, far, far + near)]
    )
    stack, _ = lax.optimization_barrier((stack, term_b))
    parts_b = lax.all_to_all(term_b, hid, split_axis=0, concat_axis=0, tiled=True)
    pieces = [(stack, [0, near * cores, far * cores, (far + near) * cores])]
    mask = near // 2
    while mask:
        arrived = [
            (lax.ppermute(piece, "chip", across(mask)), [q ^ (mask * cores) for q in order])
            for piece, order in pieces
        ]
        pieces = pieces + arrived
        mask //= 2
    pieces = pieces + [
        (lax.ppermute(piece, "core", other), [q ^ 1 for q in order]) for piece, order in pieces
    ]
    gathered = [piece for piece, _ in pieces]
    orders = [order for _, order in pieces]

    out_chunks = pl.pallas_call(
        functools.partial(
            output_kernel, orders=orders, block=block, picks=picks, rank=rank, runs=runs, n=n
        ),
        out_shape=jax.ShapeDtypeStruct((n, block, chunk), bf16),
        in_specs=[pl.BlockSpec(memory_space=pltpu.SMEM)] * 2 + [vmem] * (len(gathered) + 3),
        out_specs=anywhere,
        scratch_shapes=[
            pltpu.VMEM((n, block, chunk), bf16),
            pltpu.SemaphoreType.DMA((n,)),
        ],
        compiler_params=pltpu.CompilerParams(vmem_limit_bytes=vmem_limit),
        name="output_columns",
    )(ids, active, *gathered, dm, do, adapter_output_maps)
    out_cols = lax.all_to_all(out_chunks, hid, split_axis=0, concat_axis=0, tiled=True)
    if chunk % 128 == 0:
        output = pl.pallas_call(
            functools.partial(join_copies_kernel, **sizes),
            out_shape=jax.ShapeDtypeStruct((block, model), bf16),
            in_specs=[vmem],
            out_specs=anywhere,
            scratch_shapes=[pltpu.SemaphoreType.DMA((n,))],
            compiler_params=pltpu.CompilerParams(vmem_limit_bytes=8 * 1024 * 1024),
            name="join_columns",
        )(out_cols)
    else:
        output = call(
            functools.partial(join_columns_kernel, **sizes),
            "join_columns",
            jax.ShapeDtypeStruct((block, model), bf16),
            (strips,),
            [pl.BlockSpec((per, block, chunk), lambda i, ids: (i, 0, 0))],
            pl.BlockSpec((block, strip), lambda i, ids: (0, i)),
            (ids,),
            (out_cols,),
        )

    maps_a = jax.ShapeDtypeStruct(adapter_input_maps.shape, f32)
    maps_b = jax.ShapeDtypeStruct(adapter_output_maps.shape, f32)
    lanes = jax.ShapeDtypeStruct((runs, block), f32)
    grad_a, grad_b, squares = call(
        functools.partial(
            gradients_kernel,
            sizes=[len(order) for order in orders],
            block=block,
            picks=picks,
            rank=rank,
            runs=runs,
            n=n,
        ),
        "gradients",
        (maps_a, maps_b, lanes),
        (1,),
        [whole(a) for a in (*gathered, dropout_tiles, parts_b)],
        [whole(maps_a), whole(maps_b), whole(lanes)],
        (ids, active, counts, seeds, jnp.array(sum(orders, []), jnp.int32)),
        (*gathered, dropout_tiles, parts_b),
    )
    squares = squares + lax.ppermute(squares, "core", other)
    mask = 1
    while mask < near:
        squares = squares + lax.ppermute(squares, "chip", across(mask))
        mask *= 2
    totals = [squares] + [
        lax.ppermute(squares, "chip", across(m)) for m in (far, near, far + near)
    ]
    totals, output = lax.optimization_barrier((totals, output))
    limit = math.sqrt(rank * (n * block + model))
    updated = call(
        functools.partial(adamw_kernel, limit=limit, runs=runs),
        "adamw",
        (maps_a,) * 3 + (maps_b,) * 3,
        (1,),
        [whole(lanes)] * len(totals) + [whole(maps_a)] * 4 + [whole(maps_b)] * 4,
        [whole(maps_a)] * 3 + [whole(maps_b)] * 3,
        (ids,),
        (
            *totals,
            adapter_input_maps,
            first_moment_input,
            second_moment_input,
            grad_a,
            adapter_output_maps,
            first_moment_output,
            second_moment_output,
            grad_b,
        ),
    )
    return (output, *updated)


def solution(mesh):
    groups, n = mesh.devices.shape
    fine = Mesh(mesh.devices.reshape(groups, n // 2, 2), ("groups", "chip", "core"))
    hid = ("chip", "core")
    rows = P(("groups",) + hid, None)
    maps = P("groups", None, hid)
    return jax.shard_map(
        body,
        mesh=fine,
        in_specs=(rows, rows, P(None, hid), P(None, hid), P(hid, None))
        + (maps,) * 6
        + (P("groups", None), P("groups"), P(), P("groups")),
        out_specs=(rows,) + (maps,) * 6,
        check_vma=False,
    )
```
